32 devices in a mesh: section: 2 (over x), tp: 4 (over y, core), ctx: 4 (over z).
Axes of the slice: x: 2, y: 2, z: 4, core: 2. Of those that a mesh axis runs over, the one named last changes fastest.
Arguments:
- tokens_in: bfloat16 [2, 8, 16384], P(None, None, 'ctx'), may hold values from -6 to 6
- norm_gain: bfloat16 [2, 16384], P('section', 'ctx'), may hold values from 0.25 to 1.75
- w_qkv: bfloat16 [2, 16384, 18432], P('section', 'ctx', 'tp'), may hold values from -0.375 to 0.375
- w_out: bfloat16 [2, 16384, 16384], P('section', 'tp', 'ctx'), may hold values from -0.046875 to 0.046875
- prefix_keys: bfloat16 [2, 8, 16384, 128], P('section', 'tp', 'ctx'), may hold values from -400 to 400
- prefix_values: bfloat16 [2, 8, 16384, 128], P('section', 'tp', 'ctx'), may hold values from -6 to 6
- suffix_keys: bfloat16 [2, 8, 8, 512, 128], P('section', 'tp', 'ctx'), may hold values from -27 to 27
- suffix_values: bfloat16 [2, 8, 8, 512, 128], P('section', 'tp', 'ctx'), may hold values from -6 to 6
- lengths: int32 [8], replicated, may hold values from 1 to 512, 2048 in all
- order: int32 [8], replicated, may hold values from 0 to 7, each once
Outputs:
- layer_out: float32 [2, 2, 8, 16384], P('section', None, 'tp', 'ctx')
The draws below stay inside these ranges and needn't reach their ends.
Inputs may be any that keep to these rules, and one draw needn't show every extreme that they name: `lengths`: some sample has 512. `order`: each sample appears in exactly one row.
All inputs are finite; a program needn't handle non-finite values.
Results may differ from the reference program's by a relative error of at most 0.014.
Values may be sent and summed in bfloat16 or wider, within the bound.
No kernel may reach another device: no remote copies, remote signals or barrier semaphores. Data moves between devices by JAX's collectives and lax.ppermute only.
A program may use at most 128 MiB of HBM per device.

```python
import math
import jax
import jax.numpy as jnp
import numpy as np
from jax import lax

D = 16384
HEADS = 128
KVH = 8
HD = 128
SMAX = 512
G = 16
LAYERS = 2
B = 8
PREFIX = 16384


def draw_w_qkv(key, part):
    group = (HEADS // KVH + 2) * HD
    column = jnp.arange(KVH * group) % group
    query_cols = HEADS // KVH * HD
    column_scale = jnp.where((column >= query_cols) & (column < query_cols + HD), 8.0, 1.0)
    shape = (LAYERS, D, KVH * group)
    base = jnp.clip(jax.random.normal(key, shape, jnp.float32), -6.0, 6.0)
    return (base * column_scale[None, None, :] * D ** (-0.5)).astype(jnp.bfloat16)


def draw_prefix_keys(key, part):
    shape = (LAYERS, KVH, PREFIX, HD)
    key_base = jax.random.fold_in(key, 11)
    base = jnp.clip(jax.random.normal(key_base, shape, jnp.float32), -6.0, 6.0) * 2.5
    return base.astype(jnp.bfloat16)


def shard_levels(own_key, dims, pieces, smallest, largest):
    level = 1.0
    for dim, shards_of in pieces:
        steps = jax.random.uniform(jax.random.fold_in(jax.random.fold_in(own_key, 6), dim), (shards_of,), jnp.float32, smallest / len(pieces), largest / len(pieces))
        level = level * jnp.repeat(jnp.exp(steps), dims[dim] // shards_of).reshape((-1,) + (1,) * (len(dims) - 1 - dim))
    return level


def split_up(amount, total, reach, slope):
    loads = [(1 << 20) // math.isqrt(grade ** slope) + 1 for grade in range(2, amount + 1)]
    spare, holding = total - reach - (amount - 1), [1] * (amount - 1)
    while spare > 0:
        free = [i for i in range(amount - 1) if holding[i] < reach]
        pool, left = sum([loads[i] for i in free]), spare
        for i in free:
            extra = min(reach - holding[i], max(1, left * loads[i] // pool), spare)
            holding[i] = holding[i] + extra
            spare = spare - extra
    return np.array([reach] + holding)


def uneven(rng, amount, total, limit, skew):
    if amount == 2:
        one = jax.random.randint(rng, (), max(1, total - limit), min(limit, total - 1) + 1)
        return jnp.stack([one, total - one])
    sizes = jnp.asarray(split_up(amount, total, limit, skew), jnp.int32)
    twos = (amount - 1) // 2
    source_of, sink = sizes[1:1 + 2 * twos:2], sizes[2:2 + 2 * twos:2]
    room = jnp.minimum(source_of - 1, limit - sink)
    moved = jax.random.randint(jax.random.fold_in(rng, 1), (twos,), 0, 1 << 20) % (room + 1)
    sizes = sizes.at[1:1 + 2 * twos:2].set(source_of - moved).at[2:2 + 2 * twos:2].set(sink + moved)
    return sizes[jax.random.permutation(jax.random.fold_in(rng, 2), amount)]


def normal_values(own_key, dims, scale, limit, split=(), held_as=jnp.bfloat16):
    factor_of = shard_levels(own_key, dims, split, -0.22, 0.18) if split else 1.0
    drawn = jax.random.normal(own_key, dims, jnp.float32) * scale * factor_of
    return jnp.minimum(jnp.maximum(drawn, -limit), limit).astype(held_as)


def setup_inputs(seed: int = 0) -> dict:
    arg_keys = jax.random.split(jax.random.key(seed), 11)
    return {
        "tokens_in": normal_values(arg_keys[0], (2, B, D), 1.0, 6.0, ((2, 4),)),
        "norm_gain": jnp.clip(1.0 + 0.15 * jax.random.normal(arg_keys[1], (LAYERS, D), jnp.float32), 0.25, 1.75).astype(jnp.bfloat16),
        "w_qkv": draw_w_qkv(jax.random.fold_in(arg_keys[10], 71), 0),
        "w_out": normal_values(arg_keys[3], (LAYERS, HEADS * HD, D), (HEADS * HD) ** -0.5, 0.046875, ((0, 2), (1, 4), (2, 4))),
        "prefix_keys": draw_prefix_keys(jax.random.fold_in(arg_keys[10], 71), 0),
        "prefix_values": normal_values(arg_keys[5], (LAYERS, KVH, PREFIX, HD), 1.0, 6.0, ((0, 2), (1, 4), (2, 4))),
        "suffix_keys": normal_values(arg_keys[6], (LAYERS, KVH, B, SMAX, HD), 4.5, 27.0, ((0, 2), (1, 4), (2, 4))),
        "suffix_values": normal_values(arg_keys[7], (LAYERS, KVH, B, SMAX, HD), 1.0, 6.0, ((0, 2), (1, 4), (2, 4))),
        "lengths": uneven(arg_keys[8], B, B * SMAX // 2, SMAX, 2).astype(jnp.int32),
        "order": jax.random.permutation(arg_keys[9], B).astype(jnp.int32),
    }


EPSILON = 1e-05
NEGATIVE = -1e+30

def rounded(values):
    return lax.optimization_barrier(values.astype(jnp.bfloat16)).astype(jnp.float32)

def apply_layer(hidden, layer_index, norm_gain, w_qkv, w_out, prefix_keys, prefix_values, suffix_keys, suffix_values, in_suffix, order, previous):
    row_count = hidden.shape[0]
    hidden_f = hidden.astype(jnp.float32)
    mean_sq = lax.optimization_barrier(jnp.mean(hidden_f * hidden_f, axis=1))
    scaled = (hidden_f * norm_gain[layer_index].astype(jnp.float32)[None, :]).astype(jnp.bfloat16)
    projected = jnp.dot(scaled, w_qkv[layer_index], preferred_element_type=jnp.float32) * lax.rsqrt(mean_sq + EPSILON)[:, None]
    projected = projected.astype(jnp.bfloat16).reshape(row_count, KVH, G + 2, HD)
    queries = projected[:, :, :G].transpose(1, 0, 2, 3)
    keys_new = projected[:, :, G].transpose(1, 0, 2)
    values_new = projected[:, :, G + 1].transpose(1, 0, 2)
    suffix_k = suffix_keys[layer_index][:, order]
    suffix_v = suffix_values[layer_index][:, order]
    has_old = previous is not None
    keys_old = previous[0] if has_old else keys_new
    values_old = previous[1] if has_old else values_new
    score_scale = HD ** (-0.5)

    def per_head(head_inputs):
        query_h, pre_k, pre_v, suf_k, suf_v, new_k, new_v, old_k, old_v = head_inputs
        query_f = query_h.astype(jnp.float32)
        pre_scores = jnp.einsum('bgd,pd->bgp', query_f, pre_k.astype(jnp.float32)) * score_scale
        suf_scores = jnp.einsum('bgd,bpd->bgp', query_f, suf_k.astype(jnp.float32)) * score_scale
        suf_scores = jnp.where(in_suffix[:, None, :], suf_scores, NEGATIVE)
        own_scores = jnp.einsum('bgd,bd->bg', query_f, new_k.astype(jnp.float32)) * score_scale
        row_max = jnp.maximum(jnp.maximum(lax.optimization_barrier(jnp.max(pre_scores, axis=2)), lax.optimization_barrier(jnp.max(suf_scores, axis=2))), own_scores)
        if has_old:
            old_scores = jnp.einsum('bgd,bd->bg', query_f, old_k.astype(jnp.float32)) * score_scale
            row_max = jnp.maximum(row_max, old_scores)
        pre_w = jnp.exp(pre_scores - row_max[..., None])
        suf_w = jnp.where(in_suffix[:, None, :], jnp.exp(suf_scores - row_max[..., None]), 0.0)
        own_w = jnp.exp(own_scores - row_max)
        totals = lax.optimization_barrier(jnp.sum(pre_w, axis=2)) + lax.optimization_barrier(jnp.sum(suf_w, axis=2)) + own_w
        summed = jnp.einsum('bgp,pd->bgd', rounded(pre_w), pre_v.astype(jnp.float32))
        summed = summed + jnp.einsum('bgp,bpd->bgd', rounded(suf_w), suf_v.astype(jnp.float32))
        summed = summed + rounded(own_w)[..., None] * new_v.astype(jnp.float32)[:, None, :]
        if has_old:
            old_w = jnp.exp(old_scores - row_max)
            totals = totals + old_w
            summed = summed + rounded(old_w)[..., None] * old_v.astype(jnp.float32)[:, None, :]
        return summed / totals[..., None]
    attention = lax.map(per_head, (queries, prefix_keys[layer_index], prefix_values[layer_index], suffix_k, suffix_v, keys_new, values_new, keys_old, values_old))
    attention = attention.transpose(1, 0, 2, 3).reshape(row_count, HEADS * HD).astype(jnp.bfloat16)
    output = jnp.dot(attention, w_out[layer_index], preferred_element_type=jnp.float32)
    return (hidden_f + output, (keys_new, values_new))

def reference(tokens_in, norm_gain, w_qkv, w_out, prefix_keys, prefix_values, suffix_keys, suffix_values, lengths, order):
    sample_len = lengths[order]
    in_suffix = jnp.arange(SMAX, dtype=jnp.int32)[None, :] < sample_len[:, None]
    results = [[] for layer_index in range(LAYERS)]
    previous = [None] * LAYERS
    for step_index in range(2):
        hidden = tokens_in[step_index].astype(jnp.float32)
        for layer_index in range(LAYERS):
            hidden, fresh = apply_layer(hidden, layer_index, norm_gain, w_qkv, w_out, prefix_keys, prefix_values, suffix_keys, suffix_values, in_suffix, order, previous[layer_index])
            previous[layer_index] = fresh
            results[layer_index].append(hidden)
    return jnp.stack([jnp.stack(entries) for entries in results])
```

```python
import functools
import math

import jax
import jax.numpy as jnp
from jax import lax
from jax.experimental import pallas as pl
from jax.experimental.pallas import tpu as pltpu
from jax.sharding import PartitionSpec as P

EPSILON = 1e-05
NEGATIVE = -1e30
LANES = 128
F32 = jnp.float32
BF16 = jnp.bfloat16


def params(megabytes):
    return pltpu.CompilerParams(vmem_limit_bytes=megabytes << 20)


def whole(shape):
    return pl.BlockSpec(shape, lambda *_: (0,) * len(shape))


def split3(value):
    high = value.astype(BF16).astype(F32)
    rest = value - high
    middle = rest.astype(BF16).astype(F32)
    return high, middle, rest - middle


def divisor(size, largest):
    best = LANES
    while best * 2 <= largest and size % (best * 2) == 0:
        best *= 2
    return best


def project_kernel(chunks, depth, fresh, me_ref, x_ref, aux_ref, w_ref, *rest):
    outs, (xg_ref, sq_ref, acc_ref) = rest[:chunks], rest[chunks:]
    k, step = pl.program_id(0), pl.program_id(1)
    wide = xg_ref.shape[0] * depth

    @pl.when(jnp.logical_and(k == 0, step == 0))
    def _():
        if fresh:
            x = x_ref[...].astype(F32)
            xg = (x * aux_ref[...].astype(F32)).astype(BF16)
            squares = jnp.sum(x * x, axis=1, keepdims=True)
        else:
            turn = aux_ref[...]
            xg = jnp.dot(turn, x_ref[:, :wide], preferred_element_type=F32).astype(BF16)
            terms = jnp.dot(turn, x_ref[:, wide:], preferred_element_type=F32)
            squares = terms[:, 0:1] + terms[:, 1:2] + terms[:, 2:3]
        for i in range(xg_ref.shape[0]):
            xg_ref[i] = xg[:, i * depth : (i + 1) * depth]
        sq_ref[...] = jnp.broadcast_to(squares, sq_ref.shape)

    part = jnp.dot(xg_ref[step], w_ref[...], preferred_element_type=F32)

    @pl.when(step == 0)
    def _():
        acc_ref[...] = part

    @pl.when(step > 0)
    def _():
        acc_ref[...] += part

    width = acc_ref.shape[1]
    for i in range(chunks):

        @pl.when(jnp.logical_and(k == i, step == pl.num_programs(1) - 1))
        def _():
            outs[i][:, :width] = acc_ref[...]
            outs[i][:, width:] = sq_ref[...]


def project(x, aux, w, me, chunks, fresh):
    rows = x.shape[0]
    model, columns = w.shape[1:]
    width = columns // chunks
    depth = divisor(model, 1024)
    shape = jax.ShapeDtypeStruct((rows, width + LANES), F32)
    return pl.pallas_call(
        functools.partial(project_kernel, chunks, depth, fresh),
        out_shape=[shape] * chunks,
        grid_spec=pltpu.PrefetchScalarGridSpec(
            num_scalar_prefetch=1,
            grid=(chunks, model // depth),
            in_specs=[
                whole(x.shape),
                whole(aux.shape),
                pl.BlockSpec(
                    (None, depth, width),
                    lambda k, i, me: (0, i, lax.rem(me[0] - k + chunks, chunks)),
                ),
            ],
            out_specs=[whole(shape.shape)] * chunks,
            scratch_shapes=[
                pltpu.VMEM((model // depth, rows, depth), BF16),
                pltpu.VMEM((rows, LANES), F32),
                pltpu.VMEM((rows, width), F32),
            ],
        ),
        compiler_params=params(24),
        cost_estimate=pl.CostEstimate(
            flops=2 * rows * model * columns, bytes_accessed=2 * model * columns, transcendentals=0
        ),
    )(me, x, aux, w)


def normalize_kernel(model, *refs):
    total = refs[0][...]
    for ref in refs[1:-1]:
        total = total + ref[...]
    out_ref = refs[-1]
    width = out_ref.shape[1]
    scale = lax.rsqrt(total[:, width : width + 1] / model + EPSILON)
    out_ref[...] = (total[:, :width] * scale).astype(BF16)


def normalize(parts, model):
    rows, width = parts[0].shape
    return pl.pallas_call(
        functools.partial(normalize_kernel, model),
        out_shape=jax.ShapeDtypeStruct((rows, width - LANES), BF16),
        compiler_params=params(8),
        cost_estimate=pl.CostEstimate(
            flops=rows * width * 4, bytes_accessed=rows * width * 16, transcendentals=0
        ),
    )(*parts)


def attend_kernel(
    blocks, chunks, batch, group, me_ref, order_ref, lengths_ref, *rest
):
    parts = rest[:blocks]
    pre_k, pre_v, suf_k, suf_v = rest[blocks : blocks + 4]
    outs = rest[blocks + 4 : blocks + 4 + chunks]
    q_ref, s_ref, o_ref = rest[blocks + 4 + chunks :]
    head = pl.program_id(0)
    me = me_ref[0]
    rows, hd = q_ref.shape[1], pre_k.shape[1]
    slots = group + 2
    own = parts[0].shape[1] // hd
    scale = hd**-0.5 * math.log2(math.e)

    @pl.when(head == 0)
    def _():
        for k in range(blocks):
            at = lax.rem(me - k + blocks, blocks)
            for i in range(own):
                q_ref[at * own + i] = parts[k][:, i * hd : (i + 1) * hd]

    first = head * slots
    q = jnp.concatenate([q_ref[first + g] for g in range(group)], axis=0)
    count = group * rows
    positions = pre_k.shape[0]
    samples, depth = suf_k.shape[0], suf_k.shape[1]
    step = divisor(positions, 1024)
    sstep = divisor(depth, 1024)
    pad = -rows % LANES
    zeros = jnp.zeros((pad, hd), BF16)
    keys_new = jnp.concatenate([q_ref[first + group], zeros], axis=0)
    values_new = jnp.concatenate([q_ref[first + group + 1], zeros], axis=0)
    tail = rows + pad

    def dot_t(a, b):
        return lax.dot_general(a, b, (((1,), (1,)), ((), ())), preferred_element_type=F32)

    top = jnp.full((count, LANES), NEGATIVE, F32)

    def keep(top, scores, start):
        s_ref[:, start : start + scores.shape[1]] = scores
        for i in range(0, scores.shape[1], LANES):
            top = jnp.maximum(top, scores[:, i : i + LANES])
        return top

    def masked(scores, mask):
        bias = jnp.where(mask, 0.0, NEGATIVE)
        shaped = scores.reshape(group, rows, scores.shape[1]) + bias[None]
        return shaped.reshape(scores.shape)

    pieces = []
    start = 0
    for i in range(0, positions, step):
        top = keep(top, dot_t(q, pre_k[i : i + step]), start)
        pieces.append((start, step, pre_v, None, i))
        start += step
    for s in range(samples):
        sample = me * samples + s
        row = jnp.int32(0)
        for b in range(batch):
            row = row + jnp.where(order_ref[b] == sample, b, 0)
        length = lengths_ref[sample]
        for i in range(0, depth, sstep):
            r = lax.broadcasted_iota(jnp.int32, (rows, sstep), 0)
            p = lax.broadcasted_iota(jnp.int32, (rows, sstep), 1) + i
            mine = r == row
            for t in range(1, rows // batch):
                mine = jnp.logical_or(mine, r == row + t * batch)
            mask = jnp.logical_and(mine, p < length)
            top = keep(top, masked(dot_t(q, suf_k[s, i : i + sstep]), mask), start)
            pieces.append((start, sstep, suf_v, s, i))
            start += sstep
    r = lax.broadcasted_iota(jnp.int32, (rows, tail), 0)
    p = lax.broadcasted_iota(jnp.int32, (rows, tail), 1)
    gap = jnp.where(me == 0, r - p, -1)
    mask = gap == 0
    for t in range(1, rows // batch):
        mask = jnp.logical_or(mask, gap == t * batch)
    top = keep(top, masked(dot_t(q, keys_new), mask), start)
    pieces.append((start, tail, None, None, 0))

    row_max = jnp.max(top, axis=1, keepdims=True) * scale
    total = jnp.zeros((count, LANES), F32)
    mixed = jnp.zeros((count, hd), F32)
    for start, size, values, s, i in pieces:
        weights = jnp.exp2(s_ref[:, start : start + size] * scale - row_max)
        for lane in range(0, size, LANES):
            total = total + weights[:, lane : lane + LANES]
        if values is None:
            v = values_new
        elif s is None:
            v = values[i : i + size]
        else:
            v = values[s, i : i + size]
        mixed = mixed + jnp.dot(weights.astype(BF16), v, preferred_element_type=F32)
    total = jnp.sum(total, axis=1, keepdims=True)
    mixed = mixed * (1.0 / total)
    level = row_max + jnp.log2(total)
    terms = split3(level)

    per = o_ref.shape[2] // hd - 1
    lane = lax.broadcasted_iota(jnp.int32, (rows, LANES), 1)
    for first_head in range(0, group, per):
        at = head * (group // per) + first_head // per
        stats = jnp.zeros((rows, LANES), F32)
        for i in range(per):
            g = first_head + i
            o_ref[at, :, i * hd : (i + 1) * hd] = mixed[g * rows : (g + 1) * rows].astype(BF16)
            for n in range(3):
                stats = jnp.where(lane == n * per + i, terms[n][g * rows : (g + 1) * rows], stats)
        o_ref[at, :, per * hd :] = stats.astype(BF16)

    @pl.when(head == pl.num_programs(0) - 1)
    def _():
        for k in range(chunks):
            outs[k][...] = o_ref[lax.rem(me - k + chunks, chunks)]


def attend(parts, keys, values, suffix_keys, suffix_values, me, order, lengths, chunks, group):
    rows = parts[0].shape[0]
    heads, positions, hd = keys.shape[1:]
    samples, depth = suffix_keys.shape[2:4]
    width = heads * group * hd // chunks + LANES
    total = positions + samples * depth + rows + (-rows % LANES)
    shape = jax.ShapeDtypeStruct((rows, width), BF16)
    cache = pl.BlockSpec((None, None, positions, hd), lambda h, *_: (0, h, 0, 0))
    suffix = pl.BlockSpec((None, None, samples, depth, hd), lambda h, *_: (0, h, 0, 0, 0))
    return pl.pallas_call(
        functools.partial(attend_kernel, len(parts), chunks, order.shape[0], group),
        out_shape=[shape] * chunks,
        grid_spec=pltpu.PrefetchScalarGridSpec(
            num_scalar_prefetch=3,
            grid=(heads,),
            in_specs=[whole(part.shape) for part in parts] + [cache, cache, suffix, suffix],
            out_specs=[whole(shape.shape)] * chunks,
            scratch_shapes=[
                pltpu.VMEM((heads * (group + 2), rows, hd), BF16),
                pltpu.VMEM((group * rows, total), F32),
                pltpu.VMEM((chunks, rows, width), BF16),
            ],
        ),
        compiler_params=params(56),
        cost_estimate=pl.CostEstimate(
            flops=4 * heads * group * rows * total * hd,
            bytes_accessed=4 * heads * total * hd,
            transcendentals=heads * group * rows * total,
        ),
    )(me, order, lengths, *parts, keys, values, suffix_keys, suffix_values)


def merge_kernel(hd, *refs):
    parts, out_ref = refs[:-1], refs[-1]
    per = out_ref.shape[1] // hd
    stats = [ref[:, per * hd :].astype(F32) for ref in parts]
    for i in range(per):
        levels = [
            s[:, i : i + 1] + s[:, per + i : per + i + 1] + s[:, 2 * per + i : 2 * per + i + 1]
            for s in stats
        ]
        top = functools.reduce(jnp.maximum, levels)
        shares = [jnp.exp2(level - top) for level in levels]
        inverse = 1.0 / functools.reduce(jnp.add, shares)
        mixed = 0.0
        for ref, share in zip(parts, shares):
            mixed = mixed + ref[:, i * hd : (i + 1) * hd].astype(F32) * (share * inverse)
        out_ref[:, i * hd : (i + 1) * hd] = mixed.astype(BF16)


def merge(parts, hd):
    rows, width = parts[0].shape
    return pl.pallas_call(
        functools.partial(merge_kernel, hd),
        out_shape=jax.ShapeDtypeStruct((rows, width - LANES), BF16),
        compiler_params=params(8),
        cost_estimate=pl.CostEstimate(
            flops=rows * width * 8, bytes_accessed=rows * width * 10, transcendentals=rows * LANES
        ),
    )(*parts)


def output_kernel(blocks, per, groups, me_ref, turn_ref, *rest):
    parts = rest[:blocks]
    w_ref = rest[blocks]
    outs = rest[blocks + 1 : blocks + 1 + groups]
    a_ref, acc_ref = rest[blocks + 1 + groups :]
    step = pl.program_id(0)
    depth = a_ref.shape[2]

    @pl.when(step == 0)
    def _():
        for k in range(blocks):
            turned = jnp.dot(turn_ref[...], parts[k][...], preferred_element_type=F32).astype(BF16)
            for i in range(per):
                a_ref[k * per + i] = turned[:, i * depth : (i + 1) * depth]

    part = jnp.dot(a_ref[step], w_ref[...], preferred_element_type=F32)

    @pl.when(step == 0)
    def _():
        acc_ref[...] = part

    @pl.when(step > 0)
    def _():
        acc_ref[...] += part

    @pl.when(step == pl.num_programs(0) - 1)
    def _():
        size = outs[0].shape[0]
        stride = acc_ref.shape[0] // groups
        for k in range(groups):
            outs[k][...] = acc_ref[k * stride : k * stride + size, :]


def output(parts, turn, w, me, groups, size):
    blocks = len(parts)
    rows, width = parts[0].shape
    columns = w.shape[2]
    depth = divisor(width, 512)
    per = width // depth
    padded = turn.shape[0]
    shape = jax.ShapeDtypeStruct((size, columns), F32)
    return pl.pallas_call(
        functools.partial(output_kernel, blocks, per, groups),
        out_shape=[shape] * groups,
        grid_spec=pltpu.PrefetchScalarGridSpec(
            num_scalar_prefetch=1,
            grid=(blocks * per,),
            in_specs=[whole(turn.shape)]
            + [whole(part.shape) for part in parts]
            + [
                pl.BlockSpec(
                    (None, depth, columns),
                    lambda i, me: (0, lax.rem(me[0] - i // per + blocks, blocks) * per + i % per, 0),
                )
            ],
            out_specs=[whole(shape.shape)] * groups,
            scratch_shapes=[
                pltpu.VMEM((blocks * per, padded, depth), BF16),
                pltpu.VMEM((padded, columns), F32),
            ],
        ),
        compiler_params=params(24),
        cost_estimate=pl.CostEstimate(
            flops=2 * rows * blocks * width * columns,
            bytes_accessed=2 * blocks * width * columns,
            transcendentals=0,
        ),
    )(me, turn, *parts, w)


def add_kernel(*refs):
    parts, gain_ref, y_ref, out_ref = refs[:-3], refs[-3], refs[-2], refs[-1]
    total = parts[0][...]
    for ref in parts[1:]:
        total = total + ref[...]
    y_ref[...] = total
    wide = total.shape[1]
    out_ref[:, :wide] = (total * gain_ref[...].astype(F32)).astype(BF16)
    squares = jnp.sum(total * total, axis=1, keepdims=True)
    lane = lax.broadcasted_iota(jnp.int32, (total.shape[0], LANES), 1)
    terms = jnp.zeros((total.shape[0], LANES), F32)
    for n, term in enumerate(split3(squares)):
        terms = jnp.where(lane == n, term, terms)
    out_ref[:, wide:] = terms.astype(BF16)


def add_up(parts, gain):
    rows, width = parts[0].shape
    return pl.pallas_call(
        add_kernel,
        out_shape=[
            jax.ShapeDtypeStruct((rows, width), F32),
            jax.ShapeDtypeStruct((rows, width + LANES), BF16),
        ],
        compiler_params=params(8),
        cost_estimate=pl.CostEstimate(
            flops=rows * width * 8, bytes_accessed=rows * width * 24, transcendentals=0
        ),
    )(*parts, gain)


def back(parts, axis):
    count = lax.axis_size(axis)
    return [parts[0]] + [
        lax.ppermute(parts[k], axis, [(i, (i - k) % count) for i in range(count)])
        for k in range(1, count)
    ]


def around(part, axis):
    count = lax.axis_size(axis)
    return [part] + [
        lax.ppermute(part, axis, [(i, (i + k) % count) for i in range(count)])
        for k in range(1, count)
    ]


def on_device(
    tokens_in,
    norm_gain,
    w_qkv,
    w_out,
    prefix_keys,
    prefix_values,
    suffix_keys,
    suffix_values,
    lengths,
    order,
):
    sections = lax.axis_size("section")
    ctx, tp = lax.axis_size("ctx"), lax.axis_size("tp")
    steps, batch, columns = tokens_in.shape
    rows = steps * batch
    heads, hd = prefix_keys.shape[1], prefix_keys.shape[4 - 1]
    slots = w_qkv.shape[2] // (heads * hd)
    group = slots - 2
    model = w_qkv.shape[1] * ctx
    share = batch // tp
    size = steps * share
    section, tp_me = lax.axis_index("section"), lax.axis_index("tp")
    me = lax.axis_index("ctx").astype(jnp.int32).reshape(1)
    even = (heads * slots) % ctx == 0
    zero = jnp.zeros((1,), jnp.int32)

    stride = size + (-size % 8)
    i = jnp.arange(tp * stride)
    k, j = i // stride, i % stride
    owner = lax.rem(tp_me - k + tp, tp)
    natural = jnp.where(j < size, (j // share) * batch + owner * share + j % share, -1)
    turn = (natural[:, None] == jnp.arange(rows)[None, :]).astype(BF16)
    i = jnp.arange(tp * size)
    k, j = i // size, i % size
    owner = lax.rem(tp_me - k + tp, tp)
    natural = (j // share) * batch + owner * share + j % share
    unturn = (jnp.arange(rows)[:, None] == natural[None, :]).astype(BF16)

    mine = lax.dynamic_slice_in_dim(tokens_in, tp_me * share, share, 1)
    residual = mine.astype(F32).reshape(size, columns)
    gain = norm_gain
    next_gain = lax.ppermute(
        norm_gain, "section", [(s, (s - 1) % sections) for s in range(sections)]
    )

    x, aux = tokens_in.reshape(rows, columns), gain
    result = None
    for layer in range(sections):
        fresh = layer == 0
        if even:
            parts = back(project(x, aux, w_qkv, me, ctx, fresh), "ctx")
            parts = around(normalize(parts, model), "ctx")
        else:
            part = project(x, aux, w_qkv, zero, 1, fresh)[0]
            parts = [normalize([lax.psum(part, "ctx")], model)]
        parts = attend(
            parts, prefix_keys, prefix_values, suffix_keys, suffix_values,
            me, order, lengths, ctx, group,
        )
        parts = around(merge(back(parts, "ctx"), hd), "ctx")
        parts = back(output(parts, turn, w_out, me, tp, size), "tp")
        y, message = add_up(parts + [residual], next_gain)
        result = y if result is None else jnp.where(section == layer, y, result)
        if layer + 1 < sections:
            here, there = layer * tp, (layer + 1) * tp
            received = [
                lax.ppermute(
                    message, ("section", "tp"), [(here + n, there + (n + k) % tp) for n in range(tp)]
                )
                for k in range(tp)
            ]
            x, aux = jnp.concatenate(received, axis=0), unturn
            residual = lax.ppermute(y, "section", [(layer, layer + 1)])
    return result.reshape(1, steps, share, columns)


def solution(mesh):
    in_specs = (
        P(None, None, "ctx"),
        P("section", "ctx"),
        P("section", "ctx", "tp"),
        P("section", "tp", "ctx"),
        P("section", "tp", "ctx", None),
        P("section", "tp", "ctx", None),
        P("section", "tp", "ctx", None, None),
        P("section", "tp", "ctx", None, None),
        P(),
        P(),
    )
    out_specs = P("section", None, "tp", "ctx")
    return jax.shard_map(
        on_device, mesh=mesh, in_specs=in_specs, out_specs=out_specs, check_vma=False
    )
```

```python
import functools
import math

import jax
import jax.numpy as jnp
from jax import lax
from jax.experimental import pallas as pl
from jax.experimental.pallas import tpu as pltpu
from jax.sharding import PartitionSpec as P

EPSILON = 1e-05
NEGATIVE = -1e30
LANES = 128
F32 = jnp.float32
BF16 = jnp.bfloat16


def params(megabytes):
    return pltpu.CompilerParams(vmem_limit_bytes=megabytes << 20)


def whole(shape):
    return pl.BlockSpec(shape, lambda *_: (0,) * len(shape))


def split3(value):
    high = value.astype(BF16).astype(F32)
    rest = value - high
    middle = rest.astype(BF16).astype(F32)
    return high, middle, rest - middle


def block_depth(model):
    return divisor(model, 256)


def divisor(size, largest):
    best = LANES
    while best * 2 <= largest and size % (best * 2) == 0:
        best *= 2
    return best


def hbm():
    return pl.BlockSpec(memory_space=pltpu.HBM)


def vmem():
    return pl.BlockSpec(memory_space=pltpu.VMEM)


def smem():
    return pl.BlockSpec(memory_space=pltpu.SMEM)


def row_copy(w_ref, first, index, depth, to_ref, sem_ref):
    rows = pl.ds(pl.multiple_of((first + index) * depth, depth), depth)
    return pltpu.make_async_copy(w_ref.at[0, rows], to_ref.at[index], sem_ref.at[index])


def load_kernel(first, w_ref, after_ref, out_ref, sem_ref):
    count, depth = out_ref.shape[:2]
    for i in range(count):
        row_copy(w_ref, first, i, depth, out_ref, sem_ref).start()
    for i in range(count):
        row_copy(w_ref, first, i, depth, out_ref, sem_ref).wait()


def load(w, first, count, depth, after):
    columns = w.shape[2]
    return pl.pallas_call(
        functools.partial(load_kernel, first),
        out_shape=jax.ShapeDtypeStruct((count, depth, columns), BF16),
        in_specs=[hbm(), pl.BlockSpec(memory_space=pl.ANY)],
        out_specs=vmem(),
        scratch_shapes=[pltpu.SemaphoreType.DMA((count,))],
        compiler_params=params(26),
        cost_estimate=pl.CostEstimate(
            flops=0, bytes_accessed=2 * count * depth * columns, transcendentals=0
        ),
    )(w, after)


def each_block(apply, held, w_ref, buffer_ref, sem_ref):
    at = 0
    for part_ref in held:

        @pl.loop(0, part_ref.shape[0])
        def _(i, part_ref=part_ref, at=at):
            apply(at + i, part_ref[i])

        at += part_ref.shape[0]
    depth = buffer_ref.shape[1]

    @pl.loop(0, buffer_ref.shape[0])
    def _(i):
        row_copy(w_ref, at, i, depth, buffer_ref, sem_ref).wait()
        apply(at + i, buffer_ref[i])


def start_blocks(held, w_ref, buffer_ref, sem_ref):
    at = sum(part_ref.shape[0] for part_ref in held)
    for i in range(buffer_ref.shape[0]):
        row_copy(w_ref, at, i, buffer_ref.shape[1], buffer_ref, sem_ref).start()


def project_kernel(chunks, parts, fresh, me_ref, x_ref, aux_ref, w_ref, *rest):
    held, outs = rest[:parts], rest[parts : parts + chunks]
    xg_ref, sq_ref, acc_ref, buffer_ref, sem_ref = rest[parts + chunks :]
    start_blocks(held, w_ref, buffer_ref, sem_ref)
    blocks, rows, depth = xg_ref.shape
    wide = blocks * depth
    width = acc_ref.shape[2]
    if fresh:
        x = x_ref[...].astype(F32)
        xg = (x * aux_ref[...].astype(F32)).astype(BF16)
        squares = jnp.sum(x * x, axis=1, keepdims=True)
    else:
        turn = aux_ref[...]
        xg = jnp.dot(turn, x_ref[:, :wide], preferred_element_type=F32).astype(BF16)
        terms = jnp.dot(turn, x_ref[:, wide:], preferred_element_type=F32)
        squares = terms[:, 0:1] + terms[:, 1:2] + terms[:, 2:3]
    for i in range(blocks):
        xg_ref[i] = xg[:, i * depth : (i + 1) * depth]
    sq_ref[...] = jnp.broadcast_to(squares, sq_ref.shape)
    acc_ref[...] = jnp.zeros_like(acc_ref)

    def apply(i, w):
        part = jnp.dot(xg_ref[i], w, preferred_element_type=F32)
        for k in range(chunks):
            acc_ref[k] += part[:, k * width : (k + 1) * width]

    each_block(apply, held, w_ref, buffer_ref, sem_ref)
    me = me_ref[0]
    for k in range(chunks):
        outs[k][:, :width] = acc_ref[lax.rem(me - k + chunks, chunks)]
        outs[k][:, width:] = sq_ref[...]


def project(x, aux, w, held, me, chunks, fresh):
    rows = x.shape[0]
    model, columns = w.shape[1:]
    width = columns // chunks
    depth = block_depth(model)
    left = model // depth - sum(part.shape[0] for part in held)
    shape = jax.ShapeDtypeStruct((rows, width + LANES), F32)
    return pl.pallas_call(
        functools.partial(project_kernel, chunks, len(held), fresh),
        out_shape=[shape] * chunks,
        in_specs=[smem(), vmem(), vmem(), hbm()] + [vmem()] * len(held),
        out_specs=[vmem()] * chunks,
        scratch_shapes=[
            pltpu.VMEM((model // depth, rows, depth), BF16),
            pltpu.VMEM((rows, LANES), F32),
            pltpu.VMEM((chunks, rows, width), F32),
            pltpu.VMEM((left, depth, columns), BF16),
            pltpu.SemaphoreType.DMA((left,)),
        ],
        compiler_params=params(6 + (2 * left * depth * columns >> 20)),
        cost_estimate=pl.CostEstimate(
            flops=2 * rows * model * columns,
            bytes_accessed=2 * left * depth * columns,
            transcendentals=0,
        ),
    )(me, x, aux, w, *held)


def normalize_kernel(model, *refs):
    total = refs[0][...]
    for ref in refs[1:-1]:
        total = total + ref[...]
    out_ref = refs[-1]
    width = out_ref.shape[1]
    scale = lax.rsqrt(total[:, width : width + 1] / model + EPSILON)
    out_ref[...] = (total[:, :width] * scale).astype(BF16)


def normalize(parts, model):
    rows, width = parts[0].shape
    return pl.pallas_call(
        functools.partial(normalize_kernel, model),
        out_shape=jax.ShapeDtypeStruct((rows, width - LANES), BF16),
        compiler_params=params(8),
        cost_estimate=pl.CostEstimate(
            flops=rows * width * 4, bytes_accessed=rows * width * 16, transcendentals=0
        ),
    )(*parts)


def attend_kernel(
    blocks, chunks, batch, group, me_ref, order_ref, lengths_ref, *rest
):
    parts = rest[:blocks]
    pre_k, pre_v, suf_k, suf_v = rest[blocks : blocks + 4]
    outs = rest[blocks + 4 : blocks + 4 + chunks]
    q_ref, s_ref, o_ref = rest[blocks + 4 + chunks :]
    head = pl.program_id(0)
    me = me_ref[0]
    rows, hd = q_ref.shape[1], pre_k.shape[1]
    slots = group + 2
    own = parts[0].shape[1] // hd
    scale = hd**-0.5 * math.log2(math.e)

    @pl.when(head == 0)
    def _():
        for k in range(blocks):
            at = lax.rem(me - k + blocks, blocks)
            for i in range(own):
                q_ref[at * own + i] = parts[k][:, i * hd : (i + 1) * hd]

    first = head * slots
    q = jnp.concatenate([q_ref[first + g] for g in range(group)], axis=0)
    count = group * rows
    positions = pre_k.shape[0]
    samples, depth = suf_k.shape[0], suf_k.shape[1]
    step = divisor(positions, 1024)
    sstep = divisor(depth, 1024)
    pad = -rows % LANES
    zeros = jnp.zeros((pad, hd), BF16)
    keys_new = jnp.concatenate([q_ref[first + group], zeros], axis=0)
    values_new = jnp.concatenate([q_ref[first + group + 1], zeros], axis=0)
    tail = rows + pad

    def dot_t(a, b):
        return lax.dot_general(a, b, (((1,), (1,)), ((), ())), preferred_element_type=F32)

    top = jnp.full((count, LANES), NEGATIVE, F32)

    def keep(top, scores, start):
        s_ref[:, start : start + scores.shape[1]] = scores
        for i in range(0, scores.shape[1], LANES):
            top = jnp.maximum(top, scores[:, i : i + LANES])
        return top

    def masked(scores, mask):
        bias = jnp.where(mask, 0.0, NEGATIVE)
        shaped = scores.reshape(group, rows, scores.shape[1]) + bias[None]
        return shaped.reshape(scores.shape)

    pieces = []
    start = 0
    for i in range(0, positions, step):
        top = keep(top, dot_t(q, pre_k[i : i + step]), start)
        pieces.append((start, step, pre_v, None, i))
        start += step
    for s in range(samples):
        sample = me * samples + s
        row = jnp.int32(0)
        for b in range(batch):
            row = row + jnp.where(order_ref[b] == sample, b, 0)
        length = lengths_ref[sample]
        for i in range(0, depth, sstep):
            r = lax.broadcasted_iota(jnp.int32, (rows, sstep), 0)
            p = lax.broadcasted_iota(jnp.int32, (rows, sstep), 1) + i
            mine = r == row
            for t in range(1, rows // batch):
                mine = jnp.logical_or(mine, r == row + t * batch)
            mask = jnp.logical_and(mine, p < length)
            top = keep(top, masked(dot_t(q, suf_k[s, i : i + sstep]), mask), start)
            pieces.append((start, sstep, suf_v, s, i))
            start += sstep
    r = lax.broadcasted_iota(jnp.int32, (rows, tail), 0)
    p = lax.broadcasted_iota(jnp.int32, (rows, tail), 1)
    gap = jnp.where(me == 0, r - p, -1)
    mask = gap == 0
    for t in range(1, rows // batch):
        mask = jnp.logical_or(mask, gap == t * batch)
    top = keep(top, masked(dot_t(q, keys_new), mask), start)
    pieces.append((start, tail, None, None, 0))

    row_max = jnp.max(top, axis=1, keepdims=True) * scale
    total = jnp.zeros((count, LANES), F32)
    mixed = jnp.zeros((count, hd), F32)
    for start, size, values, s, i in pieces:
        weights = jnp.exp2(s_ref[:, start : start + size] * scale - row_max)
        for lane in range(0, size, LANES):
            total = total + weights[:, lane : lane + LANES]
        if values is None:
            v = values_new
        elif s is None:
            v = values[i : i + size]
        else:
            v = values[s, i : i + size]
        mixed = mixed + jnp.dot(weights.astype(BF16), v, preferred_element_type=F32)
    total = jnp.sum(total, axis=1, keepdims=True)
    mixed = mixed * (1.0 / total)
    level = row_max + jnp.log2(total)
    terms = split3(level)

    per = o_ref.shape[2] // hd - 1
    lane = lax.broadcasted_iota(jnp.int32, (rows, LANES), 1)
    for first_head in range(0, group, per):
        at = head * (group // per) + first_head // per
        stats = jnp.zeros((rows, LANES), F32)
        for i in range(per):
            g = first_head + i
            o_ref[at, :, i * hd : (i + 1) * hd] = mixed[g * rows : (g + 1) * rows].astype(BF16)
            for n in range(3):
                stats = jnp.where(lane == n * per + i, terms[n][g * rows : (g + 1) * rows], stats)
        o_ref[at, :, per * hd :] = stats.astype(BF16)

    @pl.when(head == pl.num_programs(0) - 1)
    def _():
        for k in range(chunks):
            outs[k][...] = o_ref[lax.rem(me - k + chunks, chunks)]


def attend(parts, keys, values, suffix_keys, suffix_values, me, order, lengths, chunks, group):
    rows = parts[0].shape[0]
    heads, positions, hd = keys.shape[1:]
    samples, depth = suffix_keys.shape[2:4]
    width = heads * group * hd // chunks + LANES
    total = positions + samples * depth + rows + (-rows % LANES)
    shape = jax.ShapeDtypeStruct((rows, width), BF16)
    cache = pl.BlockSpec((None, None, positions, hd), lambda h, *_: (0, h, 0, 0))
    suffix = pl.BlockSpec((None, None, samples, depth, hd), lambda h, *_: (0, h, 0, 0, 0))
    return pl.pallas_call(
        functools.partial(attend_kernel, len(parts), chunks, order.shape[0], group),
        out_shape=[shape] * chunks,
        grid_spec=pltpu.PrefetchScalarGridSpec(
            num_scalar_prefetch=3,
            grid=(heads,),
            in_specs=[whole(part.shape) for part in parts] + [cache, cache, suffix, suffix],
            out_specs=[whole(shape.shape)] * chunks,
            scratch_shapes=[
                pltpu.VMEM((heads * (group + 2), rows, hd), BF16),
                pltpu.VMEM((group * rows, total), F32),
                pltpu.VMEM((chunks, rows, width), BF16),
            ],
        ),
        compiler_params=params(20 if group * rows * total < 1 << 21 else 48),
        cost_estimate=pl.CostEstimate(
            flops=4 * heads * group * rows * total * hd,
            bytes_accessed=4 * heads * total * hd,
            transcendentals=heads * group * rows * total,
        ),
    )(me, order, lengths, *parts, keys, values, suffix_keys, suffix_values)


def merge_kernel(hd, *refs):
    parts, out_ref = refs[:-2], refs[-1]
    per = out_ref.shape[1] // hd
    stats = [ref[:, per * hd :].astype(F32) for ref in parts]
    for i in range(per):
        levels = [
            s[:, i : i + 1] + s[:, per + i : per + i + 1] + s[:, 2 * per + i : 2 * per + i + 1]
            for s in stats
        ]
        top = functools.reduce(jnp.maximum, levels)
        shares = [jnp.exp2(level - top) for level in levels]
        inverse = 1.0 / functools.reduce(jnp.add, shares)
        mixed = 0.0
        for ref, share in zip(parts, shares):
            mixed = mixed + ref[:, i * hd : (i + 1) * hd].astype(F32) * (share * inverse)
        out_ref[:, i * hd : (i + 1) * hd] = mixed.astype(BF16)


def merge(parts, hd, after):
    rows, width = parts[0].shape
    return pl.pallas_call(
        functools.partial(merge_kernel, hd),
        out_shape=jax.ShapeDtypeStruct((rows, width - LANES), BF16),
        in_specs=[vmem()] * len(parts) + [pl.BlockSpec(memory_space=pl.ANY)],
        compiler_params=params(8),
        cost_estimate=pl.CostEstimate(
            flops=rows * width * 8, bytes_accessed=rows * width * 10, transcendentals=rows * LANES
        ),
    )(*parts, after)


def output_kernel(blocks, groups, parts, me_ref, turn_ref, w_ref, *rest):
    mixed, held = rest[:blocks], rest[blocks : blocks + parts]
    outs = rest[blocks + parts : blocks + parts + groups]
    a_ref, acc_ref, buffer_ref, sem_ref = rest[blocks + parts + groups :]
    start_blocks(held, w_ref, buffer_ref, sem_ref)
    depth = a_ref.shape[2]
    per = mixed[0].shape[1] // depth
    me = me_ref[0]
    for k in range(blocks):
        turned = jnp.dot(turn_ref[...], mixed[k][...], preferred_element_type=F32).astype(BF16)
        at = lax.rem(me - k + blocks, blocks) * per
        for i in range(per):
            a_ref[at + i] = turned[:, i * depth : (i + 1) * depth]
    acc_ref[...] = jnp.zeros_like(acc_ref)

    def apply(i, w):
        acc_ref[...] += jnp.dot(a_ref[i], w, preferred_element_type=F32)

    each_block(apply, held, w_ref, buffer_ref, sem_ref)
    size = outs[0].shape[0]
    stride = acc_ref.shape[0] // groups
    for k in range(groups):
        outs[k][...] = acc_ref[k * stride : k * stride + size, :]


def output(mixed, turn, w, held, me, groups, size, depth):
    blocks = len(mixed)
    rows = mixed[0].shape[0]
    model, columns = w.shape[1:]
    left = model // depth - sum(part.shape[0] for part in held)
    padded = turn.shape[0]
    shape = jax.ShapeDtypeStruct((size, columns), F32)
    return pl.pallas_call(
        functools.partial(output_kernel, blocks, groups, len(held)),
        out_shape=[shape] * groups,
        in_specs=[smem(), vmem(), hbm()] + [vmem()] * (blocks + len(held)),
        out_specs=[vmem()] * groups,
        scratch_shapes=[
            pltpu.VMEM((model // depth, padded, depth), BF16),
            pltpu.VMEM((padded, columns), F32),
            pltpu.VMEM((left, depth, columns), BF16),
            pltpu.SemaphoreType.DMA((left,)),
        ],
        compiler_params=params(6 + (2 * left * depth * columns >> 20)),
        cost_estimate=pl.CostEstimate(
            flops=2 * rows * model * columns,
            bytes_accessed=2 * left * depth * columns,
            transcendentals=0,
        ),
    )(me, turn, w, *mixed, *held)


def add_kernel(*refs):
    parts, (gain_ref, _, y_ref, out_ref) = refs[:-4], refs[-4:]
    total = parts[0][...]
    for ref in parts[1:]:
        total = total + ref[...]
    y_ref[...] = total
    wide = total.shape[1]
    out_ref[:, :wide] = (total * gain_ref[...].astype(F32)).astype(BF16)
    squares = jnp.sum(total * total, axis=1, keepdims=True)
    lane = lax.broadcasted_iota(jnp.int32, (total.shape[0], LANES), 1)
    terms = jnp.zeros((total.shape[0], LANES), F32)
    for n, term in enumerate(split3(squares)):
        terms = jnp.where(lane == n, term, terms)
    out_ref[:, wide:] = terms.astype(BF16)


def add_up(parts, gain, after):
    rows, width = parts[0].shape
    return pl.pallas_call(
        add_kernel,
        out_shape=[
            jax.ShapeDtypeStruct((rows, width), F32),
            jax.ShapeDtypeStruct((rows, width + LANES), BF16),
        ],
        in_specs=[vmem()] * (len(parts) + 1) + [pl.BlockSpec(memory_space=pl.ANY)],
        compiler_params=params(8),
        cost_estimate=pl.CostEstimate(
            flops=rows * width * 8, bytes_accessed=rows * width * 24, transcendentals=0
        ),
    )(*parts, gain, after)


def back(parts, axis):
    count = lax.axis_size(axis)
    return [parts[0]] + [
        lax.ppermute(parts[k], axis, [(i, (i - k) % count) for i in range(count)])
        for k in range(1, count)
    ]


def around(part, axis):
    count = lax.axis_size(axis)
    return [part] + [
        lax.ppermute(part, axis, [(i, (i + k) % count) for i in range(count)])
        for k in range(1, count)
    ]


def on_device(
    tokens_in,
    norm_gain,
    w_qkv,
    w_out,
    prefix_keys,
    prefix_values,
    suffix_keys,
    suffix_values,
    lengths,
    order,
):
    sections = lax.axis_size("section")
    ctx, tp = lax.axis_size("ctx"), lax.axis_size("tp")
    steps, batch, columns = tokens_in.shape
    rows = steps * batch
    heads, hd = prefix_keys.shape[1], prefix_keys.shape[4 - 1]
    slots = w_qkv.shape[2] // (heads * hd)
    group = slots - 2
    model = w_qkv.shape[1] * ctx
    share = batch // tp
    size = steps * share
    section, tp_me = lax.axis_index("section"), lax.axis_index("tp")
    me = lax.axis_index("ctx").astype(jnp.int32).reshape(1)
    even = (heads * slots) % ctx == 0
    zero = jnp.zeros((1,), jnp.int32)

    stride = size + (-size % 8)
    i = jnp.arange(tp * stride)
    k, j = i // stride, i % stride
    owner = lax.rem(tp_me - k + tp, tp)
    natural = jnp.where(j < size, (j // share) * batch + owner * share + j % share, -1)
    turn = (natural[:, None] == jnp.arange(rows)[None, :]).astype(BF16)
    i = jnp.arange(tp * size)
    k, j = i // size, i % size
    owner = lax.rem(tp_me - k + tp, tp)
    natural = (j // share) * batch + owner * share + j % share
    unturn = (jnp.arange(rows)[:, None] == natural[None, :]).astype(BF16)

    mine = lax.dynamic_slice_in_dim(tokens_in, tp_me * share, share, 1)
    residual = mine.astype(F32).reshape(size, columns)
    gain = norm_gain
    next_gain = lax.ppermute(
        norm_gain, "section", [(s, (s - 1) % sections) for s in range(sections)]
    )

    x, aux = tokens_in.reshape(rows, columns), gain
    result = None
    in_depth, out_depth = block_depth(columns), divisor(w_out.shape[1] // ctx, 256)
    in_blocks, out_blocks = columns // in_depth, w_out.shape[1] // out_depth
    ready = []
    for layer in range(sections):
        fresh = layer == 0
        if even:
            sent = project(x, aux, w_qkv, ready, me, ctx, fresh)
            parts = back(sent, "ctx")
            parts = around(normalize(parts, model), "ctx")
        else:
            part = project(x, aux, w_qkv, ready, zero, 1, fresh)[0]
            parts = [normalize([lax.psum(part, "ctx")], model)]
        sent = attend(
            parts, prefix_keys, prefix_values, suffix_keys, suffix_values,
            me, order, lengths, ctx, group,
        )
        first = load(w_out, 0, out_blocks * 5 // 16, out_depth, sent[0])
        mixed = merge(back(sent, "ctx"), hd, first)
        second = load(w_out, first.shape[0], out_blocks * 5 // 16, out_depth, mixed)
        parts = around(mixed, "ctx")
        sent = output(parts, turn, w_out, [first, second], me, tp, size, out_depth)
        first = sent[0]
        if layer + 1 < sections:
            first = load(w_qkv, 0, in_blocks * 5 // 16, in_depth, sent[0])
        y, message = add_up(back(sent, "tp") + [residual], next_gain, first)
        result = y if result is None else jnp.where(section == layer, y, result)
        if layer + 1 < sections:
            here, there = layer * tp, (layer + 1) * tp
            received = [
                lax.ppermute(
                    message, ("section", "tp"), [(here + n, there + (n + k) % tp) for n in range(tp)]
                )
                for k in range(tp)
            ]
            second = load(w_qkv, first.shape[0], in_blocks * 5 // 16, in_depth, y)
            ready = [first, second]
            x, aux = jnp.concatenate(received, axis=0), unturn
            residual = lax.ppermute(y, "section", [(layer, layer + 1)])
    return result.reshape(1, steps, share, columns)


def solution(mesh):
    in_specs = (
        P(None, None, "ctx"),
        P("section", "ctx"),
        P("section", "ctx", "tp"),
        P("section", "tp", "ctx"),
        P("section", "tp", "ctx", None),
        P("section", "tp", "ctx", None),
        P("section", "tp", "ctx", None, None),
        P("section", "tp", "ctx", None, None),
        P(),
        P(),
    )
    out_specs = P("section", None, "tp", "ctx")
    return jax.shard_map(
        on_device, mesh=mesh, in_specs=in_specs, out_specs=out_specs, check_vma=False
    )
```

```python
import functools
import math

import jax
import jax.numpy as jnp
from jax import lax
from jax.experimental import pallas as pl
from jax.experimental.pallas import tpu as pltpu
from jax.sharding import PartitionSpec as P

EPSILON = 1e-05
NEGATIVE = -1e30
LANES = 128
F32 = jnp.float32
BF16 = jnp.bfloat16


def params(megabytes):
    return pltpu.CompilerParams(vmem_limit_bytes=megabytes << 20)


def whole(shape):
    return pl.BlockSpec(shape, lambda *_: (0,) * len(shape))


def split3(value):
    high = value.astype(BF16).astype(F32)
    rest = value - high
    middle = rest.astype(BF16).astype(F32)
    return high, middle, rest - middle


def stats_width(heads):
    return -(-3 * heads // LANES) * LANES


def block_depth(model):
    return divisor(model, 256)


def divisor(size, largest):
    best = LANES
    while best * 2 <= largest and size % (best * 2) == 0:
        best *= 2
    return best


def hbm():
    return pl.BlockSpec(memory_space=pltpu.HBM)


def vmem():
    return pl.BlockSpec(memory_space=pltpu.VMEM)


def smem():
    return pl.BlockSpec(memory_space=pltpu.SMEM)


def row_copy(w_ref, first, index, depth, to_ref, sem_ref):
    rows = pl.ds(pl.multiple_of((first + index) * depth, depth), depth)
    return pltpu.make_async_copy(w_ref.at[0, rows], to_ref.at[index], sem_ref.at[index])


def load_kernel(first, w_ref, after_ref, out_ref, sem_ref):
    count, depth = out_ref.shape[:2]
    for i in range(count):
        row_copy(w_ref, first, i, depth, out_ref, sem_ref).start()
    for i in range(count):
        row_copy(w_ref, first, i, depth, out_ref, sem_ref).wait()


def load(w, first, count, depth, after):
    columns = w.shape[2]
    return pl.pallas_call(
        functools.partial(load_kernel, first),
        out_shape=jax.ShapeDtypeStruct((count, depth, columns), BF16),
        in_specs=[hbm(), pl.BlockSpec(memory_space=pl.ANY)],
        out_specs=vmem(),
        scratch_shapes=[pltpu.SemaphoreType.DMA((count,))],
        compiler_params=params(26),
        cost_estimate=pl.CostEstimate(
            flops=0, bytes_accessed=2 * count * depth * columns, transcendentals=0
        ),
    )(w, after)


def each_block(apply, held, w_ref, buffer_ref, sem_ref):
    at = 0
    for part_ref in held:

        @pl.loop(0, part_ref.shape[0])
        def _(i, part_ref=part_ref, at=at):
            apply(at + i, part_ref[i])

        at += part_ref.shape[0]
    depth = buffer_ref.shape[1]

    @pl.loop(0, buffer_ref.shape[0])
    def _(i):
        row_copy(w_ref, at, i, depth, buffer_ref, sem_ref).wait()
        apply(at + i, buffer_ref[i])


def start_blocks(held, w_ref, buffer_ref, sem_ref):
    at = sum(part_ref.shape[0] for part_ref in held)
    for i in range(buffer_ref.shape[0]):
        row_copy(w_ref, at, i, buffer_ref.shape[1], buffer_ref, sem_ref).start()


def project_kernel(chunks, parts, fresh, me_ref, x_ref, aux_ref, w_ref, *rest):
    held, outs = rest[:parts], rest[parts : parts + chunks]
    xg_ref, sq_ref, acc_ref, buffer_ref, sem_ref = rest[parts + chunks :]
    start_blocks(held, w_ref, buffer_ref, sem_ref)
    blocks, rows, depth = xg_ref.shape
    wide = blocks * depth
    width = acc_ref.shape[2]
    if fresh:
        x = x_ref[...].astype(F32)
        xg = (x * aux_ref[...].astype(F32)).astype(BF16)
        squares = jnp.sum(x * x, axis=1, keepdims=True)
    else:
        turn = aux_ref[...]
        xg = jnp.dot(turn, x_ref[:, :wide], preferred_element_type=F32).astype(BF16)
        terms = jnp.dot(turn, x_ref[:, wide:], preferred_element_type=F32)
        squares = terms[:, 0:1] + terms[:, 1:2] + terms[:, 2:3]
    for i in range(blocks):
        xg_ref[i] = xg[:, i * depth : (i + 1) * depth]
    sq_ref[...] = jnp.broadcast_to(squares, sq_ref.shape)
    acc_ref[...] = jnp.zeros_like(acc_ref)

    def apply(i, w):
        part = jnp.dot(xg_ref[i], w, preferred_element_type=F32)
        for k in range(chunks):
            acc_ref[k] += part[:, k * width : (k + 1) * width]

    each_block(apply, held, w_ref, buffer_ref, sem_ref)
    me = me_ref[0]
    for k in range(chunks):
        outs[k][:, :width] = acc_ref[lax.rem(me - k + chunks, chunks)]
        outs[k][:, width:] = sq_ref[...]


def project(x, aux, w, held, me, chunks, fresh):
    rows = x.shape[0]
    model, columns = w.shape[1:]
    width = columns // chunks
    depth = block_depth(model)
    left = model // depth - sum(part.shape[0] for part in held)
    shape = jax.ShapeDtypeStruct((rows, width + LANES), F32)
    return pl.pallas_call(
        functools.partial(project_kernel, chunks, len(held), fresh),
        out_shape=[shape] * chunks,
        in_specs=[smem(), vmem(), vmem(), hbm()] + [vmem()] * len(held),
        out_specs=[vmem()] * chunks,
        scratch_shapes=[
            pltpu.VMEM((model // depth, rows, depth), BF16),
            pltpu.VMEM((rows, LANES), F32),
            pltpu.VMEM((chunks, rows, width), F32),
            pltpu.VMEM((left, depth, columns), BF16),
            pltpu.SemaphoreType.DMA((left,)),
        ],
        compiler_params=params(6 + (2 * left * depth * columns >> 20)),
        cost_estimate=pl.CostEstimate(
            flops=2 * rows * model * columns,
            bytes_accessed=2 * left * depth * columns,
            transcendentals=0,
        ),
    )(me, x, aux, w, *held)


def normalize_kernel(model, *refs):
    total = refs[0][...]
    for ref in refs[1:-2]:
        total = total + ref[...]
    out_ref = refs[-1]
    width = out_ref.shape[1]
    scale = lax.rsqrt(total[:, width : width + 1] / model + EPSILON)
    out_ref[...] = (total[:, :width] * scale).astype(BF16)


def normalize(parts, model, after):
    rows, width = parts[0].shape
    return pl.pallas_call(
        functools.partial(normalize_kernel, model),
        out_shape=jax.ShapeDtypeStruct((rows, width - LANES), BF16),
        in_specs=[vmem()] * len(parts) + [pl.BlockSpec(memory_space=pl.ANY)],
        compiler_params=params(8),
        cost_estimate=pl.CostEstimate(
            flops=rows * width * 4, bytes_accessed=rows * width * 16, transcendentals=0
        ),
    )(*parts, after)


def attend_kernel(
    blocks, batch, group, me_ref, order_ref, lengths_ref, *rest
):
    parts = rest[:blocks]
    pre_k, pre_v, suf_k, suf_v = rest[blocks : blocks + 4]
    out_ref, q_ref, s_ref, stats_ref = rest[blocks + 4 :]
    head = pl.program_id(0)
    me = me_ref[0]
    rows, hd = q_ref.shape[1], pre_k.shape[1]
    slots = group + 2
    own = parts[0].shape[1] // hd
    scale = hd**-0.5 * math.log2(math.e)

    @pl.when(head == 0)
    def _():
        for k in range(blocks):
            at = lax.rem(me - k + blocks, blocks)
            for i in range(own):
                q_ref[at * own + i] = parts[k][:, i * hd : (i + 1) * hd]

    first = head * slots
    q = jnp.concatenate([q_ref[first + g] for g in range(group)], axis=0)
    count = group * rows
    positions = pre_k.shape[0]
    samples, depth = suf_k.shape[0], suf_k.shape[1]
    step = divisor(positions, 1024)
    sstep = divisor(depth, 1024)
    pad = -rows % LANES
    zeros = jnp.zeros((pad, hd), BF16)
    keys_new = jnp.concatenate([q_ref[first + group], zeros], axis=0)
    values_new = jnp.concatenate([q_ref[first + group + 1], zeros], axis=0)
    tail = rows + pad

    def dot_t(a, b):
        return lax.dot_general(a, b, (((1,), (1,)), ((), ())), preferred_element_type=F32)

    top = jnp.full((count, LANES), NEGATIVE, F32)

    def keep(top, scores, start):
        s_ref[:, start : start + scores.shape[1]] = scores
        for i in range(0, scores.shape[1], LANES):
            top = jnp.maximum(top, scores[:, i : i + LANES])
        return top

    def masked(scores, mask):
        bias = jnp.where(mask, 0.0, NEGATIVE)
        shaped = scores.reshape(group, rows, scores.shape[1]) + bias[None]
        return shaped.reshape(scores.shape)

    pieces = []
    start = 0
    for i in range(0, positions, step):
        top = keep(top, dot_t(q, pre_k[i : i + step]), start)
        pieces.append((start, step, pre_v, None, i))
        start += step
    for s in range(samples):
        sample = me * samples + s
        row = jnp.int32(0)
        for b in range(batch):
            row = row + jnp.where(order_ref[b] == sample, b, 0)
        length = lengths_ref[sample]
        for i in range(0, depth, sstep):
            r = lax.broadcasted_iota(jnp.int32, (rows, sstep), 0)
            p = lax.broadcasted_iota(jnp.int32, (rows, sstep), 1) + i
            mine = r == row
            for t in range(1, rows // batch):
                mine = jnp.logical_or(mine, r == row + t * batch)
            mask = jnp.logical_and(mine, p < length)
            top = keep(top, masked(dot_t(q, suf_k[s, i : i + sstep]), mask), start)
            pieces.append((start, sstep, suf_v, s, i))
            start += sstep
    r = lax.broadcasted_iota(jnp.int32, (rows, tail), 0)
    p = lax.broadcasted_iota(jnp.int32, (rows, tail), 1)
    gap = jnp.where(me == 0, r - p, -1)
    mask = gap == 0
    for t in range(1, rows // batch):
        mask = jnp.logical_or(mask, gap == t * batch)
    top = keep(top, masked(dot_t(q, keys_new), mask), start)
    pieces.append((start, tail, None, None, 0))

    row_max = jnp.max(top, axis=1, keepdims=True) * scale
    total = jnp.zeros((count, LANES), F32)
    mixed = jnp.zeros((count, hd), F32)
    for start, size, values, s, i in pieces:
        weights = jnp.exp2(s_ref[:, start : start + size] * scale - row_max)
        for lane in range(0, size, LANES):
            total = total + weights[:, lane : lane + LANES]
        if values is None:
            v = values_new
        elif s is None:
            v = values[i : i + size]
        else:
            v = values[s, i : i + size]
        mixed = mixed + jnp.dot(weights.astype(BF16), v, preferred_element_type=F32)
    total = jnp.sum(total, axis=1, keepdims=True)
    mixed = mixed * (1.0 / total)
    level = row_max + jnp.log2(total)
    terms = split3(level)

    heads = pl.num_programs(0) * group
    mixed = mixed.astype(BF16)
    lane = lax.broadcasted_iota(jnp.int32, stats_ref.shape, 1) - first_lane(head, group)
    stats = jnp.where(head == 0, 0.0, stats_ref[...])
    for g in range(group):
        at = pl.multiple_of((head * group + g) * hd, hd)
        out_ref[:, pl.ds(at, hd)] = mixed[g * rows : (g + 1) * rows]
        for n in range(3):
            stats = jnp.where(lane == n * heads + g, terms[n][g * rows : (g + 1) * rows], stats)
    stats_ref[...] = stats
    out_ref[:, out_ref.shape[1] - stats.shape[1] :] = stats.astype(BF16)


def first_lane(head, group):
    return head * group


def attend(parts, keys, values, suffix_keys, suffix_values, me, order, lengths, group):
    rows = parts[0].shape[0]
    heads, positions, hd = keys.shape[1:]
    samples, depth = suffix_keys.shape[2:4]
    stats = stats_width(heads * group)
    width = heads * group * hd + stats
    total = positions + samples * depth + rows + (-rows % LANES)
    shape = jax.ShapeDtypeStruct((rows, width), BF16)
    cache = pl.BlockSpec((None, None, positions, hd), lambda h, *_: (0, h, 0, 0))
    suffix = pl.BlockSpec((None, None, samples, depth, hd), lambda h, *_: (0, h, 0, 0, 0))
    return pl.pallas_call(
        functools.partial(attend_kernel, len(parts), order.shape[0], group),
        out_shape=shape,
        grid_spec=pltpu.PrefetchScalarGridSpec(
            num_scalar_prefetch=3,
            grid=(heads,),
            in_specs=[whole(part.shape) for part in parts] + [cache, cache, suffix, suffix],
            out_specs=whole(shape.shape),
            scratch_shapes=[
                pltpu.VMEM((heads * (group + 2), rows, hd), BF16),
                pltpu.VMEM((group * rows, total), F32),
                pltpu.VMEM((rows, stats), F32),
            ],
        ),
        compiler_params=params(20 if group * rows * total < 1 << 21 else 48),
        cost_estimate=pl.CostEstimate(
            flops=4 * heads * group * rows * total * hd,
            bytes_accessed=4 * heads * total * hd,
            transcendentals=heads * group * rows * total,
        ),
    )(me, order, lengths, *parts, keys, values, suffix_keys, suffix_values)


def merge(parts, heads, hd, store):
    stats = [ref[:, heads * hd :].astype(F32) for ref in parts]
    levels = [
        s[:, :heads] + s[:, heads : 2 * heads] + s[:, 2 * heads : 3 * heads] for s in stats
    ]
    top = functools.reduce(jnp.maximum, levels)
    shares = [jnp.exp2(level - top) for level in levels]
    inverse = 1.0 / functools.reduce(jnp.add, shares)
    shares = [share * inverse for share in shares]
    for h in range(heads):
        mixed = 0.0
        for ref, share in zip(parts, shares):
            mixed = mixed + ref[:, h * hd : (h + 1) * hd].astype(F32) * share[:, h : h + 1]
        store(h, mixed.astype(BF16))


def output_kernel(blocks, groups, parts, hd, turn_ref, w_ref, *rest):
    mixed, held = rest[:blocks], rest[blocks : blocks + parts]
    outs = rest[blocks + parts : blocks + parts + groups]
    m_ref, a_ref, acc_ref, buffer_ref, sem_ref = rest[blocks + parts + groups :]
    start_blocks(held, w_ref, buffer_ref, sem_ref)
    depth = a_ref.shape[2]

    def store(h, value):
        m_ref[:, h * hd : (h + 1) * hd] = value

    merge(mixed, m_ref.shape[1] // hd, hd, store)
    for i in range(a_ref.shape[0]):
        turned = jnp.dot(
            turn_ref[...], m_ref[:, i * depth : (i + 1) * depth], preferred_element_type=F32
        )
        a_ref[i] = turned.astype(BF16)
    acc_ref[...] = jnp.zeros_like(acc_ref)

    def apply(i, w):
        acc_ref[...] += jnp.dot(a_ref[i], w, preferred_element_type=F32)

    each_block(apply, held, w_ref, buffer_ref, sem_ref)
    size = outs[0].shape[0]
    for k in range(groups):
        outs[k][...] = acc_ref[k * size : (k + 1) * size, :].astype(BF16)


def output(mixed, turn, w, held, groups, hd):
    blocks = len(mixed)
    rows = mixed[0].shape[0]
    model, columns = w.shape[1:]
    depth = block_depth(model)
    left = model // depth - sum(part.shape[0] for part in held)
    shape = jax.ShapeDtypeStruct((rows // groups, columns), BF16)
    return pl.pallas_call(
        functools.partial(output_kernel, blocks, groups, len(held), hd),
        out_shape=[shape] * groups,
        in_specs=[vmem(), hbm()] + [vmem()] * (blocks + len(held)),
        out_specs=[vmem()] * groups,
        scratch_shapes=[
            pltpu.VMEM((rows, model), BF16),
            pltpu.VMEM((model // depth, rows, depth), BF16),
            pltpu.VMEM((rows, columns), F32),
            pltpu.VMEM((left, depth, columns), BF16),
            pltpu.SemaphoreType.DMA((left,)),
        ],
        compiler_params=params(6 + (2 * left * depth * columns >> 20)),
        cost_estimate=pl.CostEstimate(
            flops=2 * rows * model * columns,
            bytes_accessed=2 * left * depth * columns,
            transcendentals=0,
        ),
    )(turn, w, *mixed, *held)


def add(parts, residual):
    total = parts[0][...].astype(F32)
    for ref in parts[1:]:
        total = total + ref[...].astype(F32)
    return total + residual


def residual_of(refs, size):
    if len(refs) == 1:
        return refs[0][...]
    turn_ref, tokens_ref = refs
    return jnp.dot(turn_ref[:size], tokens_ref[...], preferred_element_type=F32)


def add_kernel(count, *refs):
    parts, rest, (gain_ref, _, y_ref, out_ref) = refs[:count], refs[count:-4], refs[-4:]
    total = add(parts, residual_of(rest, y_ref.shape[0]))
    y_ref[...] = total
    wide = total.shape[1]
    out_ref[:, :wide] = (total * gain_ref[...].astype(F32)).astype(BF16)
    squares = jnp.sum(total * total, axis=1, keepdims=True)
    lane = lax.broadcasted_iota(jnp.int32, (total.shape[0], LANES), 1)
    terms = jnp.zeros((total.shape[0], LANES), F32)
    for n, term in enumerate(split3(squares)):
        terms = jnp.where(lane == n, term, terms)
    out_ref[:, wide:] = terms.astype(BF16)


def add_up(parts, residual, gain, after):
    rows, width = parts[0].shape
    return pl.pallas_call(
        functools.partial(add_kernel, len(parts)),
        out_shape=[
            jax.ShapeDtypeStruct((rows, width), F32),
            jax.ShapeDtypeStruct((rows, width + LANES), BF16),
        ],
        in_specs=[vmem()] * (len(parts) + len(residual) + 1)
        + [pl.BlockSpec(memory_space=pl.ANY)],
        compiler_params=params(8),
        cost_estimate=pl.CostEstimate(
            flops=rows * width * 8, bytes_accessed=rows * width * 16, transcendentals=0
        ),
    )(*parts, *residual, gain, after)


def finish_kernel(count, place_ref, *refs):
    parts, rest, (earlier_ref, out_ref) = refs[:count], refs[count:-2], refs[-2:]
    total = add(parts, residual_of(rest, earlier_ref.shape[0]))
    total = jnp.where(place_ref[0] == 1, total, earlier_ref[...])
    _, steps, share, _ = out_ref.shape
    for t in range(steps):
        first, second = (total[(2 * t + n) * share : (2 * t + n + 1) * share] for n in range(2))
        out_ref[0, t] = jnp.where(place_ref[1] == 0, first, second)


def finish(parts, residual, earlier, place, steps):
    rows, width = parts[0].shape
    return pl.pallas_call(
        functools.partial(finish_kernel, len(parts)),
        out_shape=jax.ShapeDtypeStruct((1, steps, rows // steps // 2, width), F32),
        in_specs=[smem()] + [vmem()] * (len(parts) + len(residual) + 1),
        out_specs=vmem(),
        compiler_params=params(8),
        cost_estimate=pl.CostEstimate(
            flops=rows * width * 8, bytes_accessed=rows * width * 16, transcendentals=0
        ),
    )(place, *parts, *residual, earlier)


def back(parts, axis):
    count = lax.axis_size(axis)
    return [parts[0]] + [
        lax.ppermute(parts[k], axis, [(i, (i - k) % count) for i in range(count)])
        for k in range(1, count)
    ]


def around(part, axis):
    count = lax.axis_size(axis)
    return [part] + [
        lax.ppermute(part, axis, [(i, (i + k) % count) for i in range(count)])
        for k in range(1, count)
    ]


def on_device(
    tokens_in,
    norm_gain,
    w_qkv,
    w_out,
    prefix_keys,
    prefix_values,
    suffix_keys,
    suffix_values,
    lengths,
    order,
):
    sections = lax.axis_size("section")
    ctx, tp = lax.axis_size("ctx"), lax.axis_size("tp")
    steps, batch, columns = tokens_in.shape
    rows = steps * batch
    heads, hd = prefix_keys.shape[1], prefix_keys.shape[4 - 1]
    slots = w_qkv.shape[2] // (heads * hd)
    group = slots - 2
    model = w_qkv.shape[1] * ctx
    share = batch // tp
    groups = tp // 2
    size = rows // groups
    section, tp_me = lax.axis_index("section"), lax.axis_index("tp")
    pair = tp_me // 2
    me = lax.axis_index("ctx").astype(jnp.int32).reshape(1)
    even = (heads * slots) % ctx == 0
    zero = jnp.zeros((1,), jnp.int32)

    i = jnp.arange(rows)
    owner, j = jnp.bitwise_xor(pair, i // size), i % size
    natural = (j // (2 * share)) * batch + owner * 2 * share + j % (2 * share)
    turn = (natural[:, None] == jnp.arange(rows)[None, :]).astype(BF16)
    unturn = (jnp.arange(rows)[:, None] == natural[None, :]).astype(BF16)

    next_gain = lax.ppermute(
        norm_gain, "section", [(s, (s - 1) % sections) for s in range(sections)]
    )

    x, aux, after = tokens_in.reshape(rows, columns), norm_gain, next_gain
    residual = (turn, x)
    result = None
    in_depth, out_depth = block_depth(columns), block_depth(w_out.shape[1])
    in_blocks, out_blocks = columns // in_depth, w_out.shape[1] // out_depth
    ready = []
    for layer in range(sections):
        fresh = layer == 0
        if even:
            sent = project(x, aux, w_qkv, ready, me, ctx, fresh)
            parts = back(sent, "ctx")
            parts = around(normalize(parts, model, after), "ctx")
        else:
            part = project(x, aux, w_qkv, ready, zero, 1, fresh)[0]
            parts = [normalize([lax.psum(part, "ctx")], model, after)]
        sent = attend(
            parts, prefix_keys, prefix_values, suffix_keys, suffix_values,
            me, order, lengths, group,
        )
        held = load(w_out, 0, max(1, out_blocks * 10 // 16), out_depth, sent)
        sent = output(around(sent, "ctx"), turn, w_out, [held], groups, hd)
        parts = [sent[0]] + [
            lax.ppermute(sent[k // 2], "tp", [(n, n ^ k) for n in range(tp)]) for k in range(1, tp)
        ]
        if layer + 1 == sections:
            place = jnp.stack([section == layer, tp_me % 2]).astype(jnp.int32)
            return finish(parts, residual, result, place, steps)
        first = load(w_qkv, 0, max(1, in_blocks * 5 // 16), in_depth, sent[0])
        y, message = add_up(parts, residual, next_gain, first)
        result = y if result is None else jnp.where(section == layer, y, result)
        here, there = layer * tp, (layer + 1) * tp
        received = []
        for k in range(0, tp, 2):
            pairs = [(here + n, there + (n ^ k)) for n in range(tp)]
            pairs += [(b, a) for a, b in pairs]
            received.append(lax.ppermute(message, ("section", "tp"), pairs))
        second = load(w_qkv, first.shape[0], max(1, in_blocks * 3 // 16), in_depth, y)
        ready = [first, second]
        x, aux = jnp.concatenate(received, axis=0), unturn
        residual = (lax.ppermute(y, "section", [(layer, layer + 1), (layer + 1, layer)]),)
        after = residual[0]


def solution(mesh):
    in_specs = (
        P(None, None, "ctx"),
        P("section", "ctx"),
        P("section", "ctx", "tp"),
        P("section", "tp", "ctx"),
        P("section", "tp", "ctx", None),
        P("section", "tp", "ctx", None),
        P("section", "tp", "ctx", None, None),
        P("section", "tp", "ctx", None, None),
        P(),
        P(),
    )
    out_specs = P("section", None, "tp", "ctx")
    return jax.shard_map(
        on_device, mesh=mesh, in_specs=in_specs, out_specs=out_specs, check_vma=False
    )
```

```python
import functools
import math

import jax
import jax.numpy as jnp
from jax import lax
from jax.experimental import pallas as pl
from jax.experimental.pallas import tpu as pltpu
from jax.sharding import PartitionSpec as P

EPSILON = 1e-05
NEGATIVE = -1e30
LANES = 128
F32 = jnp.float32
BF16 = jnp.bfloat16


def params(megabytes):
    return pltpu.CompilerParams(vmem_limit_bytes=megabytes << 20)


def whole(shape):
    return pl.BlockSpec(shape, lambda *_: (0,) * len(shape))


def split3(value):
    high = value.astype(BF16).astype(F32)
    rest = value - high
    middle = rest.astype(BF16).astype(F32)
    return high, middle, rest - middle


def stats_width(heads):
    return -(-3 * heads // LANES) * LANES


def block_depth(model):
    return divisor(model, 256)


def divisor(size, largest):
    best = LANES
    while best * 2 <= largest and size % (best * 2) == 0:
        best *= 2
    return best


def hbm():
    return pl.BlockSpec(memory_space=pltpu.HBM)


def vmem():
    return pl.BlockSpec(memory_space=pltpu.VMEM)


def smem():
    return pl.BlockSpec(memory_space=pltpu.SMEM)


def row_copy(w_ref, first, index, depth, to_ref, sem_ref):
    rows = pl.ds(pl.multiple_of((first + index) * depth, depth), depth)
    return pltpu.make_async_copy(w_ref.at[0, rows], to_ref.at[index], sem_ref.at[index])


def load_kernel(first, w_ref, after_ref, out_ref, sem_ref):
    count, depth = out_ref.shape[:2]
    for i in range(count):
        row_copy(w_ref, first, i, depth, out_ref, sem_ref).start()
    for i in range(count):
        row_copy(w_ref, first, i, depth, out_ref, sem_ref).wait()


def load(w, first, count, depth, after):
    columns = w.shape[2]
    return pl.pallas_call(
        functools.partial(load_kernel, first),
        out_shape=jax.ShapeDtypeStruct((count, depth, columns), BF16),
        in_specs=[hbm(), pl.BlockSpec(memory_space=pl.ANY)],
        out_specs=vmem(),
        scratch_shapes=[pltpu.SemaphoreType.DMA((count,))],
        compiler_params=params(26),
        cost_estimate=pl.CostEstimate(
            flops=0, bytes_accessed=2 * count * depth * columns, transcendentals=0
        ),
    )(w, after)


def each_block(apply, held, w_ref, buffer_ref, sem_ref):
    at = 0
    for part_ref in held:

        @pl.loop(0, part_ref.shape[0])
        def _(i, part_ref=part_ref, at=at):
            apply(at + i, part_ref[i])

        at += part_ref.shape[0]
    depth = buffer_ref.shape[1]

    @pl.loop(0, buffer_ref.shape[0])
    def _(i):
        row_copy(w_ref, at, i, depth, buffer_ref, sem_ref).wait()
        apply(at + i, buffer_ref[i])


def start_blocks(held, w_ref, buffer_ref, sem_ref):
    at = sum(part_ref.shape[0] for part_ref in held)
    for i in range(buffer_ref.shape[0]):
        row_copy(w_ref, at, i, buffer_ref.shape[1], buffer_ref, sem_ref).start()


def project_kernel(chunks, parts, fresh, me_ref, x_ref, aux_ref, w_ref, *rest):
    held, outs = rest[:parts], rest[parts : parts + chunks]
    xg_ref, sq_ref, acc_ref, buffer_ref, sem_ref = rest[parts + chunks :]
    start_blocks(held, w_ref, buffer_ref, sem_ref)
    blocks, rows, depth = xg_ref.shape
    wide = blocks * depth
    width = acc_ref.shape[2]
    if fresh:
        x = x_ref[...].astype(F32)
        xg = (x * aux_ref[...].astype(F32)).astype(BF16)
        squares = jnp.sum(x * x, axis=1, keepdims=True)
    else:
        turn = aux_ref[...]
        xg = jnp.dot(turn, x_ref[:, :wide], preferred_element_type=F32).astype(BF16)
        terms = jnp.dot(turn, x_ref[:, wide:], preferred_element_type=F32)
        squares = terms[:, 0:1] + terms[:, 1:2] + terms[:, 2:3]
    for i in range(blocks):
        xg_ref[i] = xg[:, i * depth : (i + 1) * depth]
    sq_ref[...] = jnp.broadcast_to(squares, sq_ref.shape)
    acc_ref[...] = jnp.zeros_like(acc_ref)

    def apply(i, w):
        part = jnp.dot(xg_ref[i], w, preferred_element_type=F32)
        for k in range(chunks):
            acc_ref[k] += part[:, k * width : (k + 1) * width]

    each_block(apply, held, w_ref, buffer_ref, sem_ref)
    me = me_ref[0]
    for k in range(chunks):
        outs[k][:, :width] = acc_ref[lax.rem(me - k + chunks, chunks)]
        outs[k][:, width:] = sq_ref[...]


def project(x, aux, w, held, me, chunks, fresh):
    rows = x.shape[0]
    model, columns = w.shape[1:]
    width = columns // chunks
    depth = block_depth(model)
    left = model // depth - sum(part.shape[0] for part in held)
    shape = jax.ShapeDtypeStruct((rows, width + LANES), F32)
    return pl.pallas_call(
        functools.partial(project_kernel, chunks, len(held), fresh),
        out_shape=[shape] * chunks,
        in_specs=[smem(), vmem(), vmem(), hbm()] + [vmem()] * len(held),
        out_specs=[vmem()] * chunks,
        scratch_shapes=[
            pltpu.VMEM((model // depth, rows, depth), BF16),
            pltpu.VMEM((rows, LANES), F32),
            pltpu.VMEM((chunks, rows, width), F32),
            pltpu.VMEM((left, depth, columns), BF16),
            pltpu.SemaphoreType.DMA((left,)),
        ],
        compiler_params=params(3 + (2 * left * depth * columns >> 20)),
        cost_estimate=pl.CostEstimate(
            flops=2 * rows * model * columns,
            bytes_accessed=2 * left * depth * columns,
            transcendentals=0,
        ),
    )(me, x, aux, w, *held)


def normalize_kernel(model, *refs):
    total = refs[0][...]
    for ref in refs[1:-2]:
        total = total + ref[...]
    out_ref = refs[-1]
    width = out_ref.shape[1]
    scale = lax.rsqrt(total[:, width : width + 1] / model + EPSILON)
    out_ref[...] = (total[:, :width] * scale).astype(BF16)


def normalize(parts, model, after):
    rows, width = parts[0].shape
    return pl.pallas_call(
        functools.partial(normalize_kernel, model),
        out_shape=jax.ShapeDtypeStruct((rows, width - LANES), BF16),
        in_specs=[vmem()] * len(parts) + [pl.BlockSpec(memory_space=pl.ANY)],
        compiler_params=params(8),
        cost_estimate=pl.CostEstimate(
            flops=rows * width * 4, bytes_accessed=rows * width * 16, transcendentals=0
        ),
    )(*parts, after)


def attend_kernel(
    blocks, batch, group, me_ref, order_ref, lengths_ref, *rest
):
    parts = rest[:blocks]
    sources = rest[blocks : blocks + 4]
    out_ref, q_ref, s_ref, stats_ref, *caches, sem_ref = rest[blocks + 4 :]
    heads = caches[0].shape[0]

    def cache_copy(n, head):
        return pltpu.make_async_copy(sources[n].at[0, head], caches[n].at[head], sem_ref.at[n, head])

    for n in range(4):
        cache_copy(n, 0).start()
    me = me_ref[0]
    hd = q_ref.shape[2]
    own = parts[0].shape[1] // hd
    for k in range(blocks):
        at = lax.rem(me - k + blocks, blocks)
        for i in range(own):
            q_ref[at * own + i] = parts[k][:, i * hd : (i + 1) * hd]

    @pl.loop(0, heads)
    def _(head):
        def following():
            @pl.when(head + 1 < heads)
            def _():
                for n in range(4):
                    cache_copy(n, head + 1).start()

        attend_head(
            head, me, batch, group, order_ref, lengths_ref, *[cache.at[head] for cache in caches],
            lambda n: cache_copy(n, head).wait(),
            following,
            heads * group, out_ref, q_ref, s_ref, stats_ref,
        )


def attend_head(
    head, me, batch, group, order_ref, lengths_ref, pre_k, suf_k, pre_v, suf_v, wait, following,
    heads, out_ref, q_ref, s_ref, stats_ref,
):
    rows, hd = q_ref.shape[1], pre_k.shape[1]
    scale = hd**-0.5 * math.log2(math.e)
    slots = group + 2
    first = head * slots
    q = jnp.concatenate([q_ref[first + g] for g in range(group)], axis=0)
    count = group * rows
    positions = pre_k.shape[0]
    samples, depth = suf_k.shape[0], suf_k.shape[1]
    step = divisor(positions, 1024)
    sstep = divisor(depth, 1024)
    pad = -rows % LANES
    zeros = jnp.zeros((pad, hd), BF16)
    keys_new = jnp.concatenate([q_ref[first + group], zeros], axis=0)
    values_new = jnp.concatenate([q_ref[first + group + 1], zeros], axis=0)
    tail = rows + pad

    def dot_t(a, b):
        return lax.dot_general(a, b, (((1,), (1,)), ((), ())), preferred_element_type=F32)

    top = jnp.full((count, LANES), NEGATIVE, F32)

    def keep(top, scores, start):
        s_ref[:, start : start + scores.shape[1]] = scores
        for i in range(0, scores.shape[1], LANES):
            top = jnp.maximum(top, scores[:, i : i + LANES])
        return top

    def masked(scores, mask):
        bias = jnp.where(mask, 0.0, NEGATIVE)
        shaped = scores.reshape(group, rows, scores.shape[1]) + bias[None]
        return shaped.reshape(scores.shape)

    pieces = []
    start = 0
    wait(0)
    for i in range(0, positions, step):
        top = keep(top, dot_t(q, pre_k[i : i + step]), start)
        pieces.append((start, step, pre_v, None, i))
        start += step
    wait(1)
    for s in range(samples):
        sample = me * samples + s
        row = jnp.int32(0)
        for b in range(batch):
            row = row + jnp.where(order_ref[b] == sample, b, 0)
        length = lengths_ref[sample]
        for i in range(0, depth, sstep):
            r = lax.broadcasted_iota(jnp.int32, (rows, sstep), 0)
            p = lax.broadcasted_iota(jnp.int32, (rows, sstep), 1) + i
            mine = r == row
            for t in range(1, rows // batch):
                mine = jnp.logical_or(mine, r == row + t * batch)
            mask = jnp.logical_and(mine, p < length)
            top = keep(top, masked(dot_t(q, suf_k[s, i : i + sstep]), mask), start)
            pieces.append((start, sstep, suf_v, s, i))
            start += sstep
    r = lax.broadcasted_iota(jnp.int32, (rows, tail), 0)
    p = lax.broadcasted_iota(jnp.int32, (rows, tail), 1)
    gap = jnp.where(me == 0, r - p, -1)
    mask = gap == 0
    for t in range(1, rows // batch):
        mask = jnp.logical_or(mask, gap == t * batch)
    top = keep(top, masked(dot_t(q, keys_new), mask), start)
    pieces.append((start, tail, None, None, 0))

    row_max = jnp.max(top, axis=1, keepdims=True) * scale
    total = jnp.zeros((count, LANES), F32)
    mixed = jnp.zeros((count, hd), F32)
    wait(2)
    wait(3)
    following()
    for start, size, values, s, i in pieces:
        weights = jnp.exp2(s_ref[:, start : start + size] * scale - row_max)
        for lane in range(0, size, LANES):
            total = total + weights[:, lane : lane + LANES]
        if values is None:
            v = values_new
        elif s is None:
            v = values[i : i + size]
        else:
            v = values[s, i : i + size]
        mixed = mixed + jnp.dot(weights.astype(BF16), v, preferred_element_type=F32)
    total = jnp.sum(total, axis=1, keepdims=True)
    mixed = mixed * (1.0 / total)
    level = row_max + jnp.log2(total)
    terms = split3(level)

    mixed = mixed.astype(BF16)
    lane = lax.broadcasted_iota(jnp.int32, stats_ref.shape, 1) - first_lane(head, group)
    stats = jnp.where(head == 0, 0.0, stats_ref[...])
    for g in range(group):
        at = pl.multiple_of((head * group + g) * hd, hd)
        out_ref[:, pl.ds(at, hd)] = mixed[g * rows : (g + 1) * rows]
        for n in range(3):
            stats = jnp.where(lane == n * heads + g, terms[n][g * rows : (g + 1) * rows], stats)
    stats_ref[...] = stats
    out_ref[:, out_ref.shape[1] - stats.shape[1] :] = stats.astype(BF16)


def first_lane(head, group):
    return head * group


def attend(parts, keys, values, suffix_keys, suffix_values, me, order, lengths, group, limit):
    rows = parts[0].shape[0]
    heads, positions, hd = keys.shape[1:]
    samples, depth = suffix_keys.shape[2:4]
    stats = stats_width(heads * group)
    width = heads * group * hd + stats
    total = positions + samples * depth + rows + (-rows % LANES)
    shape = jax.ShapeDtypeStruct((rows, width), BF16)
    return pl.pallas_call(
        functools.partial(attend_kernel, len(parts), order.shape[0], group),
        out_shape=shape,
        in_specs=[smem()] * 3 + [vmem()] * len(parts) + [hbm()] * 4,
        out_specs=vmem(),
        scratch_shapes=[
            pltpu.VMEM((heads * (group + 2), rows, hd), BF16),
            pltpu.VMEM((group * rows, total), F32),
            pltpu.VMEM((rows, stats), F32),
            pltpu.VMEM((heads, positions, hd), BF16),
            pltpu.VMEM((heads, samples, depth, hd), BF16),
            pltpu.VMEM((heads, positions, hd), BF16),
            pltpu.VMEM((heads, samples, depth, hd), BF16),
            pltpu.SemaphoreType.DMA((4, heads)),
        ],
        compiler_params=params(limit),
        cost_estimate=pl.CostEstimate(
            flops=4 * heads * group * rows * total * hd,
            bytes_accessed=4 * heads * total * hd,
            transcendentals=heads * group * rows * total,
        ),
    )(me, order, lengths, *parts, keys, suffix_keys, values, suffix_values)


def merge(parts, heads, hd, store):
    stats = [ref[:, heads * hd :].astype(F32) for ref in parts]
    levels = [
        s[:, :heads] + s[:, heads : 2 * heads] + s[:, 2 * heads : 3 * heads] for s in stats
    ]
    top = functools.reduce(jnp.maximum, levels)
    shares = [jnp.exp2(level - top) for level in levels]
    inverse = 1.0 / functools.reduce(jnp.add, shares)
    shares = [share * inverse for share in shares]
    for h in range(heads):
        mixed = 0.0
        for ref, share in zip(parts, shares):
            mixed = mixed + ref[:, h * hd : (h + 1) * hd].astype(F32) * share[:, h : h + 1]
        store(h, mixed.astype(BF16))


def output_kernel(blocks, groups, parts, hd, turn_ref, w_ref, *rest):
    mixed, held = rest[:blocks], rest[blocks : blocks + parts]
    outs = rest[blocks + parts : blocks + parts + groups]
    m_ref, a_ref, acc_ref, buffer_ref, sem_ref = rest[blocks + parts + groups :]
    start_blocks(held, w_ref, buffer_ref, sem_ref)
    depth = a_ref.shape[2]

    def store(h, value):
        m_ref[:, h * hd : (h + 1) * hd] = value

    merge(mixed, m_ref.shape[1] // hd, hd, store)
    for i in range(a_ref.shape[0]):
        turned = jnp.dot(
            turn_ref[...], m_ref[:, i * depth : (i + 1) * depth], preferred_element_type=F32
        )
        a_ref[i] = turned.astype(BF16)
    acc_ref[...] = jnp.zeros_like(acc_ref)

    def apply(i, w):
        acc_ref[...] += jnp.dot(a_ref[i], w, preferred_element_type=F32)

    each_block(apply, held, w_ref, buffer_ref, sem_ref)
    size = outs[0].shape[0]
    for k in range(groups):
        outs[k][...] = acc_ref[k * size : (k + 1) * size, :].astype(BF16)


def output(mixed, turn, w, held, groups, hd):
    blocks = len(mixed)
    rows = mixed[0].shape[0]
    model, columns = w.shape[1:]
    depth = block_depth(model)
    left = model // depth - sum(part.shape[0] for part in held)
    shape = jax.ShapeDtypeStruct((rows // groups, columns), BF16)
    return pl.pallas_call(
        functools.partial(output_kernel, blocks, groups, len(held), hd),
        out_shape=[shape] * groups,
        in_specs=[vmem(), hbm()] + [vmem()] * (blocks + len(held)),
        out_specs=[vmem()] * groups,
        scratch_shapes=[
            pltpu.VMEM((rows, model), BF16),
            pltpu.VMEM((model // depth, rows, depth), BF16),
            pltpu.VMEM((rows, columns), F32),
            pltpu.VMEM((left, depth, columns), BF16),
            pltpu.SemaphoreType.DMA((left,)),
        ],
        compiler_params=params(6 + (2 * left * depth * columns >> 20)),
        cost_estimate=pl.CostEstimate(
            flops=2 * rows * model * columns,
            bytes_accessed=2 * left * depth * columns,
            transcendentals=0,
        ),
    )(turn, w, *mixed, *held)


def add(parts, residual):
    total = parts[0][...].astype(F32)
    for ref in parts[1:]:
        total = total + ref[...].astype(F32)
    return total + residual


def residual_of(refs, size):
    if len(refs) == 1:
        return refs[0][...]
    turn_ref, tokens_ref = refs
    return jnp.dot(turn_ref[:size], tokens_ref[...], preferred_element_type=F32)


def add_kernel(count, *refs):
    parts, rest, (gain_ref, _, y_ref, out_ref) = refs[:count], refs[count:-4], refs[-4:]
    total = add(parts, residual_of(rest, y_ref.shape[0]))
    y_ref[...] = total
    wide = total.shape[1]
    out_ref[:, :wide] = (total * gain_ref[...].astype(F32)).astype(BF16)
    squares = jnp.sum(total * total, axis=1, keepdims=True)
    lane = lax.broadcasted_iota(jnp.int32, (total.shape[0], LANES), 1)
    terms = jnp.zeros((total.shape[0], LANES), F32)
    for n, term in enumerate(split3(squares)):
        terms = jnp.where(lane == n, term, terms)
    out_ref[:, wide:] = terms.astype(BF16)


def add_up(parts, residual, gain, after):
    rows, width = parts[0].shape
    return pl.pallas_call(
        functools.partial(add_kernel, len(parts)),
        out_shape=[
            jax.ShapeDtypeStruct((rows, width), F32),
            jax.ShapeDtypeStruct((rows, width + LANES), BF16),
        ],
        in_specs=[vmem()] * (len(parts) + len(residual) + 1)
        + [pl.BlockSpec(memory_space=pl.ANY)],
        compiler_params=params(8),
        cost_estimate=pl.CostEstimate(
            flops=rows * width * 8, bytes_accessed=rows * width * 16, transcendentals=0
        ),
    )(*parts, *residual, gain, after)


def finish_kernel(count, place_ref, *refs):
    parts, rest, (earlier_ref, out_ref) = refs[:count], refs[count:-2], refs[-2:]
    total = add(parts, residual_of(rest, earlier_ref.shape[0]))
    total = jnp.where(place_ref[0] == 1, total, earlier_ref[...])
    _, steps, share, _ = out_ref.shape
    for t in range(steps):
        first, second = (total[(2 * t + n) * share : (2 * t + n + 1) * share] for n in range(2))
        out_ref[0, t] = jnp.where(place_ref[1] == 0, first, second)


def finish(parts, residual, earlier, place, steps):
    rows, width = parts[0].shape
    return pl.pallas_call(
        functools.partial(finish_kernel, len(parts)),
        out_shape=jax.ShapeDtypeStruct((1, steps, rows // steps // 2, width), F32),
        in_specs=[smem()] + [vmem()] * (len(parts) + len(residual) + 1),
        out_specs=vmem(),
        compiler_params=params(8),
        cost_estimate=pl.CostEstimate(
            flops=rows * width * 8, bytes_accessed=rows * width * 16, transcendentals=0
        ),
    )(place, *parts, *residual, earlier)


def back(parts, axis):
    count = lax.axis_size(axis)
    return [parts[0]] + [
        lax.ppermute(parts[k], axis, [(i, (i - k) % count) for i in range(count)])
        for k in range(1, count)
    ]


def around(part, axis):
    count = lax.axis_size(axis)
    return [part] + [
        lax.ppermute(part, axis, [(i, (i + k) % count) for i in range(count)])
        for k in range(1, count)
    ]


def on_device(
    tokens_in,
    norm_gain,
    w_qkv,
    w_out,
    prefix_keys,
    prefix_values,
    suffix_keys,
    suffix_values,
    lengths,
    order,
):
    sections = lax.axis_size("section")
    ctx, tp = lax.axis_size("ctx"), lax.axis_size("tp")
    steps, batch, columns = tokens_in.shape
    rows = steps * batch
    heads, hd = prefix_keys.shape[1], prefix_keys.shape[4 - 1]
    slots = w_qkv.shape[2] // (heads * hd)
    group = slots - 2
    model = w_qkv.shape[1] * ctx
    share = batch // tp
    groups = tp // 2
    size = rows // groups
    section, tp_me = lax.axis_index("section"), lax.axis_index("tp")
    pair = tp_me // 2
    me = lax.axis_index("ctx").astype(jnp.int32).reshape(1)
    even = (heads * slots) % ctx == 0
    zero = jnp.zeros((1,), jnp.int32)

    i = jnp.arange(rows)
    owner, j = jnp.bitwise_xor(pair, i // size), i % size
    natural = (j // (2 * share)) * batch + owner * 2 * share + j % (2 * share)
    turn = (natural[:, None] == jnp.arange(rows)[None, :]).astype(BF16)
    unturn = (jnp.arange(rows)[:, None] == natural[None, :]).astype(BF16)

    next_gain = lax.ppermute(
        norm_gain, "section", [(s, (s - 1) % sections) for s in range(sections)]
    )
    x, aux, after = tokens_in.reshape(rows, columns), norm_gain, next_gain
    residual = (turn, x)
    result = None
    in_depth, out_depth = block_depth(columns), block_depth(w_out.shape[1])
    in_blocks, out_blocks = columns // in_depth, w_out.shape[1] // out_depth
    ready = []
    for layer in range(sections):
        fresh = layer == 0
        last = layer + 1 == sections
        parts = project(x, aux, w_qkv, ready, me if even else zero, ctx if even else 1, fresh)
        if not fresh:
            y, own = lax.optimization_barrier((y, parts[0]))
            parts = [own, *parts[1:]]
            after = own
            residual = (
                lax.ppermute(y, "section", [(layer - 1, layer), (layer, layer - 1)]),
            )
        if even:
            parts = around(normalize(back(parts, "ctx"), model, after), "ctx")
        else:
            parts = [normalize([lax.psum(parts[0], "ctx")], model, after)]
        sent = attend(
            parts, prefix_keys, prefix_values, suffix_keys, suffix_values,
            me, order, lengths, group, 52 if fresh else 34,
        )
        held = load(w_out, 0, max(1, out_blocks * 10 // 16), out_depth, sent)
        sent = output(around(sent, "ctx"), turn, w_out, [held], groups, hd)
        parts = [sent[0]] + [
            lax.ppermute(sent[k // 2], "tp", [(n, n ^ k) for n in range(tp)]) for k in range(1, tp)
        ]
        if last:
            place = jnp.stack([section == layer, tp_me % 2]).astype(jnp.int32)
            return finish(parts, residual, result, place, steps)
        first = load(w_qkv, 0, max(1, in_blocks * 4 // 16), in_depth, sent[0])
        y, message = add_up(parts, residual, next_gain, first)
        result = y if result is None else jnp.where(section == layer, y, result)
        here, there = layer * tp, (layer + 1) * tp
        received = []
        for k in range(0, tp, 2):
            pairs = [(here + n, there + (n ^ k)) for n in range(tp)]
            pairs += [(b, a) for a, b in pairs]
            received.append(lax.ppermute(message, ("section", "tp"), pairs))
        second = load(w_qkv, first.shape[0], max(1, in_blocks * 3 // 16), in_depth, y)
        ready = [first, second]
        x, aux = jnp.concatenate(received, axis=0), unturn


def solution(mesh):
    in_specs = (
        P(None, None, "ctx"),
        P("section", "ctx"),
        P("section", "ctx", "tp"),
        P("section", "tp", "ctx"),
        P("section", "tp", "ctx", None),
        P("section", "tp", "ctx", None),
        P("section", "tp", "ctx", None, None),
        P("section", "tp", "ctx", None, None),
        P(),
        P(),
    )
    out_specs = P("section", None, "tp", "ctx")
    return jax.shard_map(
        on_device, mesh=mesh, in_specs=in_specs, out_specs=out_specs, check_vma=False
    )
```

```python
import functools
import math

import jax
import jax.numpy as jnp
from jax import lax
from jax.experimental import pallas as pl
from jax.experimental.pallas import tpu as pltpu
from jax.sharding import PartitionSpec as P

EPSILON = 1e-05
NEGATIVE = -1e30
LANES = 128
F32 = jnp.float32
BF16 = jnp.bfloat16


def params(megabytes):
    return pltpu.CompilerParams(vmem_limit_bytes=megabytes << 20)


def whole(shape):
    return pl.BlockSpec(shape, lambda *_: (0,) * len(shape))


def split3(value):
    high = value.astype(BF16).astype(F32)
    rest = value - high
    middle = rest.astype(BF16).astype(F32)
    return high, middle, rest - middle


def stats_width(heads):
    return -(-3 * heads // LANES) * LANES


def block_depth(model):
    return divisor(model, 256)


def divisor(size, largest):
    best = LANES
    while best * 2 <= largest and size % (best * 2) == 0:
        best *= 2
    return best


def hbm():
    return pl.BlockSpec(memory_space=pltpu.HBM)


def vmem():
    return pl.BlockSpec(memory_space=pltpu.VMEM)


def smem():
    return pl.BlockSpec(memory_space=pltpu.SMEM)


def row_copy(w_ref, first, index, depth, to_ref, sem_ref):
    rows = pl.ds(pl.multiple_of((first + index) * depth, depth), depth)
    return pltpu.make_async_copy(w_ref.at[0, rows], to_ref.at[index], sem_ref.at[index])


def load_kernel(first, w_ref, after_ref, out_ref, sem_ref):
    count, depth = out_ref.shape[:2]
    for i in range(count):
        row_copy(w_ref, first, i, depth, out_ref, sem_ref).start()
    for i in range(count):
        row_copy(w_ref, first, i, depth, out_ref, sem_ref).wait()


def load(w, first, count, depth, after):
    columns = w.shape[2]
    return pl.pallas_call(
        functools.partial(load_kernel, first),
        out_shape=jax.ShapeDtypeStruct((count, depth, columns), BF16),
        in_specs=[hbm(), pl.BlockSpec(memory_space=pl.ANY)],
        out_specs=vmem(),
        scratch_shapes=[pltpu.SemaphoreType.DMA((count,))],
        compiler_params=params(26),
        cost_estimate=pl.CostEstimate(
            flops=0, bytes_accessed=2 * count * depth * columns, transcendentals=0
        ),
    )(w, after)


def each_block(apply, held, w_ref, buffer_ref, sem_ref):
    at = 0
    for part_ref in held:

        @pl.loop(0, part_ref.shape[0])
        def _(i, part_ref=part_ref, at=at):
            apply(at + i, part_ref[i])

        at += part_ref.shape[0]
    depth = buffer_ref.shape[1]

    @pl.loop(0, buffer_ref.shape[0])
    def _(i):
        row_copy(w_ref, at, i, depth, buffer_ref, sem_ref).wait()
        apply(at + i, buffer_ref[i])


def start_blocks(held, w_ref, buffer_ref, sem_ref):
    at = sum(part_ref.shape[0] for part_ref in held)
    for i in range(buffer_ref.shape[0]):
        row_copy(w_ref, at, i, buffer_ref.shape[1], buffer_ref, sem_ref).start()


def project_kernel(chunks, parts, fresh, me_ref, x_ref, aux_ref, w_ref, *rest):
    held, outs = rest[:parts], rest[parts : parts + chunks]
    xg_ref, sq_ref, acc_ref, buffer_ref, sem_ref = rest[parts + chunks :]
    start_blocks(held, w_ref, buffer_ref, sem_ref)
    blocks, rows, depth = xg_ref.shape
    wide = blocks * depth
    width = acc_ref.shape[2]
    if fresh:
        x = x_ref[...].astype(F32)
        xg = (x * aux_ref[...].astype(F32)).astype(BF16)
        squares = jnp.sum(x * x, axis=1, keepdims=True)
    else:
        turn = aux_ref[...]
        xg = jnp.dot(turn, x_ref[:, :wide], preferred_element_type=F32).astype(BF16)
        terms = jnp.dot(turn, x_ref[:, wide:], preferred_element_type=F32)
        squares = terms[:, 0:1] + terms[:, 1:2] + terms[:, 2:3]
    for i in range(blocks):
        xg_ref[i] = xg[:, i * depth : (i + 1) * depth]
    sq_ref[...] = jnp.broadcast_to(squares, sq_ref.shape)
    acc_ref[...] = jnp.zeros_like(acc_ref)

    def apply(i, w):
        part = jnp.dot(xg_ref[i], w, preferred_element_type=F32)
        for k in range(chunks):
            acc_ref[k] += part[:, k * width : (k + 1) * width]

    each_block(apply, held, w_ref, buffer_ref, sem_ref)
    me = me_ref[0]
    for k in range(chunks):
        outs[k][:, :width] = acc_ref[lax.rem(me - k + chunks, chunks)]
        outs[k][:, width:] = sq_ref[...]


def project(x, aux, w, held, me, chunks, fresh):
    rows = x.shape[0]
    model, columns = w.shape[1:]
    width = columns // chunks
    depth = block_depth(model)
    left = model // depth - sum(part.shape[0] for part in held)
    shape = jax.ShapeDtypeStruct((rows, width + LANES), F32)
    return pl.pallas_call(
        functools.partial(project_kernel, chunks, len(held), fresh),
        out_shape=[shape] * chunks,
        in_specs=[smem(), vmem(), vmem(), hbm()] + [vmem()] * len(held),
        out_specs=[vmem()] * chunks,
        scratch_shapes=[
            pltpu.VMEM((model // depth, rows, depth), BF16),
            pltpu.VMEM((rows, LANES), F32),
            pltpu.VMEM((chunks, rows, width), F32),
            pltpu.VMEM((left, depth, columns), BF16),
            pltpu.SemaphoreType.DMA((left,)),
        ],
        compiler_params=params(3 + (2 * left * depth * columns >> 20)),
        cost_estimate=pl.CostEstimate(
            flops=2 * rows * model * columns,
            bytes_accessed=2 * left * depth * columns,
            transcendentals=0,
        ),
    )(me, x, aux, w, *held)


def normalize_kernel(model, *refs):
    total = refs[0][...]
    for ref in refs[1:-2]:
        total = total + ref[...]
    out_ref = refs[-1]
    width = out_ref.shape[1]
    scale = lax.rsqrt(total[:, width : width + 1] / model + EPSILON)
    out_ref[...] = (total[:, :width] * scale).astype(BF16)


def normalize(parts, model, after):
    rows, width = parts[0].shape
    return pl.pallas_call(
        functools.partial(normalize_kernel, model),
        out_shape=jax.ShapeDtypeStruct((rows, width - LANES), BF16),
        in_specs=[vmem()] * len(parts) + [pl.BlockSpec(memory_space=pl.ANY)],
        compiler_params=params(8),
        cost_estimate=pl.CostEstimate(
            flops=rows * width * 4, bytes_accessed=rows * width * 16, transcendentals=0
        ),
    )(*parts, after)


def attend_kernel(
    blocks, batch, group, me_ref, order_ref, lengths_ref, *rest
):
    parts = rest[:blocks]
    sources = rest[blocks : blocks + 4]
    out_ref, q_ref, s_ref, stats_ref, *caches, sem_ref = rest[blocks + 4 :]
    heads = caches[0].shape[0]

    def cache_copy(n, head):
        return pltpu.make_async_copy(sources[n].at[0, head], caches[n].at[head], sem_ref.at[n, head])

    for n in range(4):
        cache_copy(n, 0).start()
    me = me_ref[0]
    hd = q_ref.shape[2]
    own = parts[0].shape[1] // hd
    for k in range(blocks):
        at = lax.rem(me - k + blocks, blocks)
        for i in range(own):
            q_ref[at * own + i] = parts[k][:, i * hd : (i + 1) * hd]

    @pl.loop(0, heads)
    def _(head):
        def following():
            @pl.when(head + 1 < heads)
            def _():
                for n in range(4):
                    cache_copy(n, head + 1).start()

        attend_head(
            head, me, batch, group, order_ref, lengths_ref, *[cache.at[head] for cache in caches],
            lambda n: cache_copy(n, head).wait(),
            following,
            heads * group, out_ref, q_ref, s_ref, stats_ref,
        )


def attend_head(
    head, me, batch, group, order_ref, lengths_ref, pre_k, suf_k, pre_v, suf_v, wait, following,
    heads, out_ref, q_ref, s_ref, stats_ref,
):
    rows, hd = q_ref.shape[1], pre_k.shape[1]
    scale = hd**-0.5 * math.log2(math.e)
    slots = group + 2
    first = head * slots
    q = jnp.concatenate([q_ref[first + g] for g in range(group)], axis=0)
    count = group * rows
    positions = pre_k.shape[0]
    samples, depth = suf_k.shape[0], suf_k.shape[1]
    step = divisor(positions, 1024)
    sstep = divisor(depth, 1024)
    pad = -rows % LANES
    zeros = jnp.zeros((pad, hd), BF16)
    keys_new = jnp.concatenate([q_ref[first + group], zeros], axis=0)
    values_new = jnp.concatenate([q_ref[first + group + 1], zeros], axis=0)
    tail = rows + pad

    def dot_t(a, b):
        return lax.dot_general(a, b, (((1,), (1,)), ((), ())), preferred_element_type=F32)

    top = jnp.full((count, LANES), NEGATIVE, F32)

    def keep(top, scores, start):
        s_ref[:, start : start + scores.shape[1]] = scores
        for i in range(0, scores.shape[1], LANES):
            top = jnp.maximum(top, scores[:, i : i + LANES])
        return top

    def masked(scores, mask):
        bias = jnp.where(mask, 0.0, NEGATIVE)
        shaped = scores.reshape(group, rows, scores.shape[1]) + bias[None]
        return shaped.reshape(scores.shape)

    pieces = []
    start = 0
    wait(0)
    for i in range(0, positions, step):
        top = keep(top, dot_t(q, pre_k[i : i + step]), start)
        pieces.append((start, step, pre_v, None, i))
        start += step
    wait(1)
    for s in range(samples):
        sample = me * samples + s
        row = jnp.int32(0)
        for b in range(batch):
            row = row + jnp.where(order_ref[b] == sample, b, 0)
        length = lengths_ref[sample]
        for i in range(0, depth, sstep):
            r = lax.broadcasted_iota(jnp.int32, (rows, sstep), 0)
            p = lax.broadcasted_iota(jnp.int32, (rows, sstep), 1) + i
            mine = r == row
            for t in range(1, rows // batch):
                mine = jnp.logical_or(mine, r == row + t * batch)
            mask = jnp.logical_and(mine, p < length)
            top = keep(top, masked(dot_t(q, suf_k[s, i : i + sstep]), mask), start)
            pieces.append((start, sstep, suf_v, s, i))
            start += sstep
    r = lax.broadcasted_iota(jnp.int32, (rows, tail), 0)
    p = lax.broadcasted_iota(jnp.int32, (rows, tail), 1)
    gap = jnp.where(me == 0, r - p, -1)
    mask = gap == 0
    for t in range(1, rows // batch):
        mask = jnp.logical_or(mask, gap == t * batch)
    top = keep(top, masked(dot_t(q, keys_new), mask), start)
    pieces.append((start, tail, None, None, 0))

    row_max = jnp.max(top, axis=1, keepdims=True) * scale
    total = jnp.zeros((count, LANES), F32)
    mixed = jnp.zeros((count, hd), F32)
    wait(2)
    wait(3)
    following()
    for start, size, values, s, i in pieces:
        weights = jnp.exp2(s_ref[:, start : start + size] * scale - row_max)
        for lane in range(0, size, LANES):
            total = total + weights[:, lane : lane + LANES]
        if values is None:
            v = values_new
        elif s is None:
            v = values[i : i + size]
        else:
            v = values[s, i : i + size]
        mixed = mixed + jnp.dot(weights.astype(BF16), v, preferred_element_type=F32)
    total = jnp.sum(total, axis=1, keepdims=True)
    mixed = mixed * (1.0 / total)
    level = row_max + jnp.log2(total)
    terms = split3(level)

    mixed = mixed.astype(BF16)
    lane = lax.broadcasted_iota(jnp.int32, stats_ref.shape, 1) - first_lane(head, group)
    stats = jnp.where(head == 0, 0.0, stats_ref[...])
    for g in range(group):
        at = pl.multiple_of((head * group + g) * hd, hd)
        out_ref[:, pl.ds(at, hd)] = mixed[g * rows : (g + 1) * rows]
        for n in range(3):
            stats = jnp.where(lane == n * heads + g, terms[n][g * rows : (g + 1) * rows], stats)
    stats_ref[...] = stats
    out_ref[:, out_ref.shape[1] - stats.shape[1] :] = stats.astype(BF16)


def first_lane(head, group):
    return head * group


def attend(parts, keys, values, suffix_keys, suffix_values, me, order, lengths, group, limit):
    rows = parts[0].shape[0]
    heads, positions, hd = keys.shape[1:]
    samples, depth = suffix_keys.shape[2:4]
    stats = stats_width(heads * group)
    width = heads * group * hd + stats
    total = positions + samples * depth + rows + (-rows % LANES)
    shape = jax.ShapeDtypeStruct((rows, width), BF16)
    return pl.pallas_call(
        functools.partial(attend_kernel, len(parts), order.shape[0], group),
        out_shape=shape,
        in_specs=[smem()] * 3 + [vmem()] * len(parts) + [hbm()] * 4,
        out_specs=vmem(),
        scratch_shapes=[
            pltpu.VMEM((heads * (group + 2), rows, hd), BF16),
            pltpu.VMEM((group * rows, total), F32),
            pltpu.VMEM((rows, stats), F32),
            pltpu.VMEM((heads, positions, hd), BF16),
            pltpu.VMEM((heads, samples, depth, hd), BF16),
            pltpu.VMEM((heads, positions, hd), BF16),
            pltpu.VMEM((heads, samples, depth, hd), BF16),
            pltpu.SemaphoreType.DMA((4, heads)),
        ],
        compiler_params=params(limit),
        cost_estimate=pl.CostEstimate(
            flops=4 * heads * group * rows * total * hd,
            bytes_accessed=4 * heads * total * hd,
            transcendentals=heads * group * rows * total,
        ),
    )(me, order, lengths, *parts, keys, suffix_keys, values, suffix_values)


def merge(parts, heads, hd, store):
    stats = [ref[:, heads * hd :].astype(F32) for ref in parts]
    levels = [
        s[:, :heads] + s[:, heads : 2 * heads] + s[:, 2 * heads : 3 * heads] for s in stats
    ]
    top = functools.reduce(jnp.maximum, levels)
    shares = [jnp.exp2(level - top) for level in levels]
    inverse = 1.0 / functools.reduce(jnp.add, shares)
    shares = [share * inverse for share in shares]
    for h in range(heads):
        mixed = 0.0
        for ref, share in zip(parts, shares):
            mixed = mixed + ref[:, h * hd : (h + 1) * hd].astype(F32) * share[:, h : h + 1]
        store(h, mixed.astype(BF16))


def output_kernel(blocks, groups, parts, hd, turn_ref, w_ref, *rest):
    mixed, held = rest[:blocks], rest[blocks : blocks + parts]
    outs = rest[blocks + parts : blocks + parts + groups]
    m_ref, a_ref, acc_ref, buffer_ref, sem_ref = rest[blocks + parts + groups :]
    start_blocks(held, w_ref, buffer_ref, sem_ref)
    depth = a_ref.shape[2]

    def store(h, value):
        m_ref[:, h * hd : (h + 1) * hd] = value

    merge(mixed, m_ref.shape[1] // hd, hd, store)
    for i in range(a_ref.shape[0]):
        turned = jnp.dot(
            turn_ref[...], m_ref[:, i * depth : (i + 1) * depth], preferred_element_type=F32
        )
        a_ref[i] = turned.astype(BF16)
    acc_ref[...] = jnp.zeros_like(acc_ref)

    def apply(i, w):
        acc_ref[...] += jnp.dot(a_ref[i], w, preferred_element_type=F32)

    each_block(apply, held, w_ref, buffer_ref, sem_ref)
    size = outs[0].shape[0]
    for k in range(groups):
        outs[k][...] = acc_ref[k * size : (k + 1) * size, :].astype(BF16)


def output(mixed, turn, w, held, groups, hd):
    blocks = len(mixed)
    rows = mixed[0].shape[0]
    model, columns = w.shape[1:]
    depth = block_depth(model)
    left = model // depth - sum(part.shape[0] for part in held)
    shape = jax.ShapeDtypeStruct((rows // groups, columns), BF16)
    return pl.pallas_call(
        functools.partial(output_kernel, blocks, groups, len(held), hd),
        out_shape=[shape] * groups,
        in_specs=[vmem(), hbm()] + [vmem()] * (blocks + len(held)),
        out_specs=[vmem()] * groups,
        scratch_shapes=[
            pltpu.VMEM((rows, model), BF16),
            pltpu.VMEM((model // depth, rows, depth), BF16),
            pltpu.VMEM((rows, columns), F32),
            pltpu.VMEM((left, depth, columns), BF16),
            pltpu.SemaphoreType.DMA((left,)),
        ],
        compiler_params=params(6 + (2 * left * depth * columns >> 20)),
        cost_estimate=pl.CostEstimate(
            flops=2 * rows * model * columns,
            bytes_accessed=2 * left * depth * columns,
            transcendentals=0,
        ),
    )(turn, w, *mixed, *held)


def add(parts, residual):
    total = parts[0][...].astype(F32)
    for ref in parts[1:]:
        total = total + ref[...].astype(F32)
    return total + residual


def residual_of(refs, size):
    if len(refs) == 1:
        return refs[0][...]
    turn_ref, tokens_ref = refs
    return jnp.dot(turn_ref[:size], tokens_ref[...], preferred_element_type=F32)


def add_kernel(count, *refs):
    parts, rest, (gain_ref, _, y_ref, out_ref) = refs[:count], refs[count:-4], refs[-4:]
    total = add(parts, residual_of(rest, y_ref.shape[0]))
    y_ref[...] = total
    wide = total.shape[1]
    out_ref[:, :wide] = (total * gain_ref[...].astype(F32)).astype(BF16)
    squares = jnp.sum(total * total, axis=1, keepdims=True)
    lane = lax.broadcasted_iota(jnp.int32, (total.shape[0], LANES), 1)
    terms = jnp.zeros((total.shape[0], LANES), F32)
    for n, term in enumerate(split3(squares)):
        terms = jnp.where(lane == n, term, terms)
    out_ref[:, wide:] = terms.astype(BF16)


def add_up(parts, residual, gain, after):
    rows, width = parts[0].shape
    return pl.pallas_call(
        functools.partial(add_kernel, len(parts)),
        out_shape=[
            jax.ShapeDtypeStruct((rows, width), F32),
            jax.ShapeDtypeStruct((rows, width + LANES), BF16),
        ],
        in_specs=[vmem()] * (len(parts) + len(residual) + 1)
        + [pl.BlockSpec(memory_space=pl.ANY)],
        compiler_params=params(8),
        cost_estimate=pl.CostEstimate(
            flops=rows * width * 8, bytes_accessed=rows * width * 16, transcendentals=0
        ),
    )(*parts, *residual, gain, after)


def finish_kernel(count, place_ref, *refs):
    parts, rest, (earlier_ref, out_ref) = refs[:count], refs[count:-2], refs[-2:]
    total = add(parts, residual_of(rest, earlier_ref.shape[0]))
    total = jnp.where(place_ref[0] == 1, total, earlier_ref[...])
    _, steps, share, _ = out_ref.shape
    for t in range(steps):
        first, second = (total[(2 * t + n) * share : (2 * t + n + 1) * share] for n in range(2))
        out_ref[0, t] = jnp.where(place_ref[1] == 0, first, second)


def finish(parts, residual, earlier, place, steps):
    rows, width = parts[0].shape
    return pl.pallas_call(
        functools.partial(finish_kernel, len(parts)),
        out_shape=jax.ShapeDtypeStruct((1, steps, rows // steps // 2, width), F32),
        in_specs=[smem()] + [vmem()] * (len(parts) + len(residual) + 1),
        out_specs=vmem(),
        compiler_params=params(8),
        cost_estimate=pl.CostEstimate(
            flops=rows * width * 8, bytes_accessed=rows * width * 16, transcendentals=0
        ),
    )(place, *parts, *residual, earlier)


def back(parts, axis):
    count = lax.axis_size(axis)
    return [parts[0]] + [
        lax.ppermute(parts[k], axis, [(i, (i - k) % count) for i in range(count)])
        for k in range(1, count)
    ]


def around(part, axis):
    count = lax.axis_size(axis)
    return [part] + [
        lax.ppermute(part, axis, [(i, (i + k) % count) for i in range(count)])
        for k in range(1, count)
    ]


def on_device(
    tokens_in,
    norm_gain,
    w_qkv,
    w_out,
    prefix_keys,
    prefix_values,
    suffix_keys,
    suffix_values,
    lengths,
    order,
):
    sections = lax.axis_size("section")
    ctx, tp = lax.axis_size("ctx"), lax.axis_size("tp")
    steps, batch, columns = tokens_in.shape
    rows = steps * batch
    heads, hd = prefix_keys.shape[1], prefix_keys.shape[4 - 1]
    slots = w_qkv.shape[2] // (heads * hd)
    group = slots - 2
    model = w_qkv.shape[1] * ctx
    share = batch // tp
    groups = tp // 2
    size = rows // groups
    section, tp_me = lax.axis_index("section"), lax.axis_index("tp")
    pair = tp_me // 2
    me = lax.axis_index("ctx").astype(jnp.int32).reshape(1)
    even = (heads * slots) % ctx == 0
    zero = jnp.zeros((1,), jnp.int32)

    i = jnp.arange(rows)
    owner, j = jnp.bitwise_xor(pair, i // size), i % size
    natural = (j // (2 * share)) * batch + owner * 2 * share + j % (2 * share)
    turn = (natural[:, None] == jnp.arange(rows)[None, :]).astype(BF16)
    unturn = (jnp.arange(rows)[:, None] == natural[None, :]).astype(BF16)

    next_gain = lax.ppermute(
        norm_gain, "section", [(s, (s - 1) % sections) for s in range(sections)]
    )
    x, aux, after = tokens_in.reshape(rows, columns), norm_gain, next_gain
    residual = (turn, x)
    result = None
    in_depth, out_depth = block_depth(columns), block_depth(w_out.shape[1])
    in_blocks, out_blocks = columns // in_depth, w_out.shape[1] // out_depth
    ready = []
    for layer in range(sections):
        fresh = layer == 0
        last = layer + 1 == sections
        parts = project(x, aux, w_qkv, ready, me if even else zero, ctx if even else 1, fresh)
        if not fresh:
            y, own = lax.optimization_barrier((y, parts[0]))
            parts = [own, *parts[1:]]
            after = own
            residual = (
                lax.ppermute(y, "section", [(layer - 1, layer), (layer, layer - 1)]),
            )
        if even:
            parts = around(normalize(back(parts, "ctx"), model, after), "ctx")
        else:
            parts = [normalize([lax.psum(parts[0], "ctx")], model, after)]
        sent = attend(
            parts, prefix_keys, prefix_values, suffix_keys, suffix_values,
            me, order, lengths, group, 52 if fresh else 34,
        )
        held = load(w_out, 0, max(1, out_blocks * 8 // 16), out_depth, sent)
        sent = output(around(sent, "ctx"), turn, w_out, [held], groups, hd)
        parts = [sent[0]] + [
            lax.ppermute(sent[k // 2], "tp", [(n, n ^ k) for n in range(tp)]) for k in range(1, tp)
        ]
        if last:
            place = jnp.stack([section == layer, tp_me % 2]).astype(jnp.int32)
            return finish(parts, residual, result, place, steps)
        first = load(w_qkv, 0, max(1, in_blocks * 3 // 16), in_depth, sent[0])
        y, message = add_up(parts, residual, next_gain, first)
        result = y if result is None else jnp.where(section == layer, y, result)
        here, there = layer * tp, (layer + 1) * tp
        received = []
        for k in range(0, tp, 2):
            pairs = [(here + n, there + (n ^ k)) for n in range(tp)]
            pairs += [(b, a) for a, b in pairs]
            received.append(lax.ppermute(message, ("section", "tp"), pairs))
        second = load(w_qkv, first.shape[0], max(1, in_blocks * 3 // 16), in_depth, y)
        ready = [first, second]
        x, aux = jnp.concatenate(received, axis=0), unturn


def solution(mesh):
    in_specs = (
        P(None, None, "ctx"),
        P("section", "ctx"),
        P("section", "ctx", "tp"),
        P("section", "tp", "ctx"),
        P("section", "tp", "ctx", None),
        P("section", "tp", "ctx", None),
        P("section", "tp", "ctx", None, None),
        P("section", "tp", "ctx", None, None),
        P(),
        P(),
    )
    out_specs = P("section", None, "tp", "ctx")
    return jax.shard_map(
        on_device, mesh=mesh, in_specs=in_specs, out_specs=out_specs, check_vma=False
    )
```
